512 devices in a mesh: tgt: 16 (over z), src: 32 (over y, x, core).
Axes of the slice: x: 4, y: 4, z: 16, core: 2. Of those that a mesh axis runs over, the one named last changes fastest.
Arguments:
- source_coef: bfloat16 [8192, 64, 128], P('src', 'tgt'), may hold values from -6 to 6
- couplings: bfloat16 [64, 64, 128], P('src'), may hold values from -0.09375 to 0.09375
- block_list: int32 [3, 16, 32, 512], P(None, 'tgt', 'src'), may hold values from 0 to 255, as said below
- block_count: int32 [16, 32], P('tgt', 'src'), may hold values from 1 to 512, as said below
Outputs:
- far_field: float32 [2048, 64, 128], P(('tgt', 'src'))
The draws below stay inside these ranges and needn't reach their ends.
Inputs may be any that keep to these rules, and one draw needn't show every extreme that they name: `block_list`: row 0 holds values below 128, row 1 below 256, row 2 below 64; each row reaches its largest value somewhere. `block_count`: some device has 512, some other device 1.
All inputs are finite; a program needn't handle non-finite values.
Results may differ from the reference program's by a relative error of at most 0.0003.
Values may be sent and summed in bfloat16 or wider, within the bound.
A program may use at most 128 MiB of HBM per device.

```python
import jax
import jax.numpy as jnp
from jax import lax

COEF = 64
RHS = 64
SROW = 256
NB_DEV = 512
TROW = 128
NS = 8192
NT = 2048
NCOUP = 64
N_TGT = 16
N_SRC = 32


def draw_block_list(key, part):
    key = jax.random.fold_in(key, 1)
    key_t, key_s, key_c, key_p = jax.random.split(key, 4)
    shape = (N_TGT, N_SRC, NB_DEV)
    total = N_TGT * N_SRC * NB_DEV
    targets = jax.random.randint(key_t, shape, 0, TROW).reshape(-1)
    sources = jax.random.randint(key_s, shape, 0, SROW).reshape(-1)
    kinds = jax.random.randint(key_c, shape, 0, NCOUP).reshape(-1)
    spots = jax.random.randint(key_p, (3,), 0, total)
    targets = targets.at[spots[0]].set(TROW - 1)
    sources = sources.at[spots[1]].set(SROW - 1)
    kinds = kinds.at[spots[2]].set(NCOUP - 1)
    stacked = jnp.stack([targets, sources, kinds], axis=0)
    return stacked.reshape(3, N_TGT, N_SRC, NB_DEV).astype(jnp.int32)


def draw_block_count(key, part):
    key = jax.random.fold_in(key, 2)
    key_r, key_p = jax.random.split(key)
    levels = jax.random.randint(key_r, (N_TGT * N_SRC,), 1, 17)
    counts = jnp.maximum(1, NB_DEV * levels * levels // 256)
    spot = jax.random.randint(key_p, (), 0, N_TGT * N_SRC)
    other = (spot + 1) % (N_TGT * N_SRC)
    counts = counts.at[other].set(1)
    counts = counts.at[spot].set(NB_DEV)
    return counts.reshape(N_TGT, N_SRC).astype(jnp.int32)


def level_of(rng, extent, cuts, smallest, high):
    level, own = 1.0, jax.random.fold_in(rng, 6)
    for dim, blocks in cuts:
        steps = jnp.exp(jax.random.uniform(jax.random.fold_in(own, dim), (blocks,), jnp.float32, smallest / len(cuts), high / len(cuts)))
        level = level * jnp.repeat(steps, extent[dim] // blocks).reshape([-1 if axis == dim else 1 for axis in range(len(extent))])
    return level


def noise(rng, extent, width, limit, cuts=(), kind=jnp.bfloat16):
    values = width * jax.random.normal(rng, extent, jnp.float32)
    if cuts:
        values = values * level_of(rng, extent, cuts, -0.22, 0.18)
    return jnp.clip(values, -limit, limit).astype(kind)


def setup_inputs(seed: int = 0) -> dict:
    keys = jax.random.split(jax.random.key(seed), 5)
    return {
        "source_coef": noise(keys[0], (NS, RHS, 2 * COEF), 1.0, 6.0, ((0, 32), (1, 16))),
        "couplings": noise(keys[1], (NCOUP, COEF, 2 * COEF), (2 * COEF * NB_DEV * N_SRC // (4 * TROW)) ** -0.5, 0.09375, ((0, 32),)),
        "block_list": draw_block_list(jax.random.fold_in(keys[4], 71), 0),
        "block_count": draw_block_count(jax.random.fold_in(keys[4], 71), 0),
    }


def reference(source_coef, couplings, block_list, block_count):
    tgt_base = (jnp.arange(N_TGT, dtype=jnp.int32) * TROW)[:, None, None]
    src_base = (jnp.arange(N_SRC, dtype=jnp.int32) * SROW)[None, :, None]
    targets = (block_list[0] + tgt_base).reshape(N_TGT * N_SRC, NB_DEV)
    sources = (block_list[1] + src_base).reshape(N_TGT * N_SRC, NB_DEV)
    kinds = jnp.broadcast_to(block_list[2], (N_TGT, N_SRC, NB_DEV)).reshape(N_TGT * N_SRC, NB_DEV)
    slots = jnp.arange(NB_DEV, dtype=jnp.int32)[None, :]
    valid = (slots < block_count.reshape(N_TGT * N_SRC, 1)).astype(jnp.float32)

    def one_device(total, items):
        target, source, kind, usable = items
        inputs = source_coef[source].astype(jnp.float32)
        blocks = couplings[kind].astype(jnp.float32)
        lower = jnp.concatenate([-blocks[:, :, COEF:], blocks[:, :, :COEF]], axis=2)
        square = jnp.concatenate([blocks, lower], axis=1)
        images = jnp.einsum("grm,gmn->grn", inputs, square, precision=lax.Precision.HIGHEST)
        images = images * usable[:, None, None]
        return total.at[target].add(images), None

    start = jnp.zeros((NT, RHS, 2 * COEF), jnp.float32)
    result, _ = lax.scan(one_device, start, (targets, sources, kinds, valid))
    return result
```

```python
import functools

import jax
import jax.numpy as jnp
from jax import lax
from jax.experimental import pallas as pl
from jax.experimental.pallas import tpu as pltpu
from jax.sharding import PartitionSpec as P

MESH = pl.DeviceIdType.MESH
NX, NY, NZ = 4, 4, 16
PLANE = NX * NY
KINDS, COEF, WIDTH = 64, 64, 128
SOURCES, ROWS = 256, 4
TARGETS, SLOTS = 128, 512
PIECES = 4
DEPTH = NZ // PIECES
HALF = DEPTH // 2
TROWS = TARGETS * ROWS
UNROLL = 8


def position(tgt):
    return lax.rem(tgt, PIECES) * DEPTH + tgt // PIECES


def exchange_kernel(
    lists, count, own, codes, table, packed,
    plane_send, plane_recv, core_send, core_recv, tgt_send, tgt_recv, local_sem,
):
    z, s = lax.axis_index("tgt"), lax.axis_index("src")
    core, chip = lax.rem(s, 2), s // 2
    x, y = lax.rem(chip, NX), chip // NX
    other = s + 1 - 2 * core

    def chip_at(dx, dy):
        return (lax.rem(y + dy + NY, NY) * NX + lax.rem(x + dx + NX, NX)) * 2 + core

    shifts = [(d % NX, d // NX) for d in range(1, PLANE)]
    barrier = pltpu.get_barrier_semaphore()
    peers = [{"src": other}]
    peers += [{"src": chip_at(dx, dy)} for dx, dy in shifts]
    peers += [{"tgt": lax.rem(z + d, NZ)} for d in range(1, NZ)]
    for peer in peers:
        pl.semaphore_signal(barrier, inc=1, device_id=peer, device_id_type=MESH)

    usable = count[0, 0]
    place = (
        lax.broadcasted_iota(jnp.int32, (4, 128), 0) * 128
        + lax.broadcasted_iota(jnp.int32, (4, 128), 1)
    )
    code = ((lists[2] * SOURCES + lists[1]) * ROWS) * 1024 + lists[0] * ROWS
    packed[pl.ds(0, 4), :] = jnp.where(place < usable, code, TROWS)
    packed[pl.ds(4, 4), :] = jnp.full((4, 128), usable, jnp.int32)

    pl.semaphore_wait(barrier, len(peers))

    copies = []
    for n, (dx, dy) in enumerate(shifts):
        copies.append(pltpu.make_async_remote_copy(
            src_ref=own, dst_ref=table.at[pl.ds(2 * s, 2)],
            send_sem=plane_send.at[n], recv_sem=plane_recv.at[n],
            device_id={"src": chip_at(dx, dy)}, device_id_type=MESH,
        ))
        copies[-1].start()
    lanes = []
    for d in range(1, NZ):
        lanes.append(pltpu.make_async_remote_copy(
            src_ref=packed, dst_ref=codes.at[z],
            send_sem=tgt_send.at[d - 1], recv_sem=tgt_recv.at[d - 1],
            device_id={"tgt": lax.rem(z + d, NZ)}, device_id_type=MESH,
        ))
        lanes[-1].start()
    keep_table = pltpu.make_async_copy(own, table.at[pl.ds(2 * s, 2)], local_sem.at[0])
    keep_table.start()
    keep_codes = pltpu.make_async_copy(packed, codes.at[z], local_sem.at[1])
    keep_codes.start()
    crossing = [pltpu.make_async_remote_copy(
        src_ref=own, dst_ref=table.at[pl.ds(2 * s, 2)],
        send_sem=core_send.at[0], recv_sem=core_recv.at[0],
        device_id={"src": other}, device_id_type=MESH,
    )]
    crossing[0].start()
    for n, (dx, dy) in enumerate(shifts):
        copies[n].wait_recv()
        owner = chip_at(-dx, -dy)
        crossing.append(pltpu.make_async_remote_copy(
            src_ref=table.at[pl.ds(2 * owner, 2)], dst_ref=table.at[pl.ds(2 * owner, 2)],
            send_sem=core_send.at[n + 1], recv_sem=core_recv.at[n + 1],
            device_id={"src": other}, device_id_type=MESH,
        ))
        crossing[-1].start()
    for copy in lanes + crossing:
        copy.wait()
    for copy in copies:
        copy.wait_send()
    keep_table.wait()
    keep_codes.wait()


def exchange(lists, count, couplings):
    hbm = pl.BlockSpec(memory_space=pl.ANY)
    return pl.pallas_call(
        exchange_kernel,
        out_shape=[
            jax.ShapeDtypeStruct((NZ, 8, 128), jnp.int32),
            jax.ShapeDtypeStruct((KINDS, COEF, WIDTH), jnp.bfloat16),
        ],
        in_specs=[
            pl.BlockSpec(memory_space=pltpu.VMEM),
            pl.BlockSpec(memory_space=pltpu.SMEM),
            pl.BlockSpec(memory_space=pltpu.VMEM),
        ],
        out_specs=[hbm, hbm],
        scratch_shapes=[
            pltpu.VMEM((8, 128), jnp.int32),
            pltpu.SemaphoreType.DMA((PLANE - 1,)),
            pltpu.SemaphoreType.DMA((PLANE - 1,)),
            pltpu.SemaphoreType.DMA((PLANE,)),
            pltpu.SemaphoreType.DMA((PLANE,)),
            pltpu.SemaphoreType.DMA((NZ - 1,)),
            pltpu.SemaphoreType.DMA((NZ - 1,)),
            pltpu.SemaphoreType.DMA((2,)),
        ],
        compiler_params=pltpu.CompilerParams(collective_id=0, has_side_effects=True),
        name="exchange",
    )(lists, count, couplings)


def apply_kernel(codes, coef, blocks, out, images, even, odd):
    tgt = pl.program_id(0)

    @pl.when(tgt == 0)
    def _():
        sign = jnp.where(
            lax.broadcasted_iota(jnp.int32, (COEF, WIDTH), 1) < COEF, -1.0, 1.0
        ).astype(jnp.float32)

        def square(kind):
            upper = blocks[kind]
            turned = pltpu.roll(upper.astype(jnp.float32), COEF, 1) * sign
            return jnp.concatenate([upper, turned.astype(jnp.bfloat16)], axis=0)

        def build(pair, carry):
            both = jnp.concatenate([square(2 * pair), square(2 * pair + 1)], axis=1)
            for part in range(2):
                rows = SOURCES * ROWS // 2
                product = jnp.dot(
                    coef[pl.ds(part * rows, rows), :], both,
                    preferred_element_type=jnp.float32,
                )
                for n in range(2):
                    start = pl.multiple_of((2 * pair + n) * SOURCES * ROWS + part * rows, rows)
                    images[pl.ds(start, rows), :] = product[:, n * WIDTH:(n + 1) * WIDTH]
            return carry

        lax.fori_loop(0, KINDS // 2, build, 0)

    even[...] = jnp.zeros_like(even)
    odd[...] = jnp.zeros_like(odd)
    groups = (codes[tgt, 4, 0] + UNROLL - 1) // UNROLL

    def add_group(group, carry):
        start = group * UNROLL
        row, column = start // 128, lax.rem(start, 128)
        for n in range(UNROLL):
            code = codes[tgt, row, column + n]
            image = lax.shift_right_logical(code, 10)
            target = jnp.bitwise_and(code, 1023)
            total = (even, odd)[n % 2]
            total[pl.ds(target, ROWS), :] += images[pl.ds(image, ROWS), :]
        return carry

    lax.fori_loop(0, groups, add_group, 0)
    for chip in range(PLANE):
        for core in range(2):
            rows = pl.ds((2 * chip + core) * 16, 16)
            out[core, 0, chip] = even[rows, :] + odd[rows, :]


def apply(codes, coef, blocks):
    return pl.pallas_call(
        apply_kernel,
        grid=(NZ,),
        out_shape=jax.ShapeDtypeStruct((2, NZ, PLANE, 16, WIDTH), jnp.float32),
        in_specs=[
            pl.BlockSpec(memory_space=pltpu.SMEM),
            pl.BlockSpec(memory_space=pltpu.VMEM),
            pl.BlockSpec(memory_space=pltpu.VMEM),
        ],
        out_specs=pl.BlockSpec(
            (2, 1, PLANE, 16, WIDTH), lambda i: (0, (i % PIECES) * DEPTH + i // PIECES, 0, 0, 0)
        ),
        scratch_shapes=[
            pltpu.VMEM((KINDS * SOURCES * ROWS, WIDTH), jnp.float32),
            pltpu.VMEM((TROWS + 8, WIDTH), jnp.float32),
            pltpu.VMEM((TROWS + 8, WIDTH), jnp.float32),
        ],
        compiler_params=pltpu.CompilerParams(
            dimension_semantics=("arbitrary",), vmem_limit_bytes=48 * 1024 * 1024
        ),
        name="apply",
    )(codes, coef, blocks)


def reduce_kernel(
    partial, result, total, partner, wide, narrow, columns,
    local_sem, pair_send, pair_recv, ring_send, ring_recv, tgt_send, tgt_recv,
):
    z, s = lax.axis_index("tgt"), lax.axis_index("src")
    core, chip = lax.rem(s, 2), s // 2
    x, y = lax.rem(chip, NX), chip // NX
    other = s + 1 - 2 * core

    def device(cy, cx):
        return {"src": (lax.rem(cy, NY) * NX + lax.rem(cx, NX)) * 2 + core}

    ahead = (device(y, x + 1), device(y + 1, x))
    behind = (device(y, x + NX - 1), device(y + NY - 1, x))
    barrier = pltpu.get_barrier_semaphore()
    peers = [{"src": other}, *ahead, *behind]
    peers += [{"tgt": lax.rem(z + d, NZ)} for d in range(1, NZ)]
    for peer in peers:
        pl.semaphore_signal(barrier, inc=1, device_id=peer, device_id_type=MESH)

    mine = []
    for p in range(PIECES):
        span = pl.ds(p * DEPTH, DEPTH)
        mine.append(pltpu.make_async_copy(
            partial.at[core, span], total.at[span], local_sem.at[p]))
        mine[-1].start()
    pl.semaphore_wait(barrier, len(peers))
    pairs = []
    for p in range(PIECES):
        span = pl.ds(p * DEPTH, DEPTH)
        pairs.append(pltpu.make_async_remote_copy(
            src_ref=partial.at[1 - core, span], dst_ref=partner.at[span],
            send_sem=pair_send.at[p], recv_sem=pair_recv.at[p],
            device_id={"src": other}, device_id_type=MESH,
        ))
        pairs[-1].start()

    here = (x, y)
    pending = []

    def cut(p, level, index, part):
        axis = (p + level) % 2
        span = pl.ds(p * DEPTH + part * HALF, HALF)
        if level == 0:
            return total.at[span, :, index] if axis == 0 else total.at[span, index]
        return total.at[span, index, x] if axis == 1 else total.at[span, y, index]

    def slot(p, level, n):
        return wide.at[p, n] if level == 0 else narrow.at[p, n]

    def send(p, level, n, ref):
        axis = (p + level) % 2
        copy = pltpu.make_async_remote_copy(
            src_ref=ref, dst_ref=slot(p, level, n),
            send_sem=ring_send.at[p, level, n], recv_sem=ring_recv.at[p, level, n],
            device_id=(ahead if n % 2 == 0 else behind)[axis], device_id_type=MESH,
        )
        copy.start()
        pending.append(copy)
        return copy

    rings = {}

    def add(ref, *others):
        value = ref[...]
        for one in others:
            value = value + one[...]
        ref[...] = value

    def first(p, level):
        me = here[(p + level) % 2]
        up, far, down = lax.rem(me + 1, 4), lax.rem(me + 2, 4), lax.rem(me + 3, 4)
        ring = {}
        ring[0] = send(p, level, 0, cut(p, level, far, 0))
        ring[1] = send(p, level, 1, cut(p, level, far, 1))
        ring[2] = send(p, level, 2, cut(p, level, up, 1))
        ring[3] = send(p, level, 3, cut(p, level, down, 0))
        rings[p, level] = ring

    def second(p, level):
        me = here[(p + level) % 2]
        up, down = lax.rem(me + 1, 4), lax.rem(me + 3, 4)
        ring = rings[p, level]
        ring[0].wait_recv()
        add(cut(p, level, up, 0), slot(p, level, 0))
        ring[4] = send(p, level, 4, cut(p, level, up, 0))
        ring[1].wait_recv()
        add(cut(p, level, down, 1), slot(p, level, 1))
        ring[5] = send(p, level, 5, cut(p, level, down, 1))

    def third(p, level):
        me = here[(p + level) % 2]
        ring = rings[p, level]
        for n in (2, 3, 4, 5):
            ring[n].wait_recv()
        add(cut(p, level, me, 0), slot(p, level, 3), slot(p, level, 4))
        add(cut(p, level, me, 1), slot(p, level, 2), slot(p, level, 5))

    def begin(p):
        mine[p].wait()
        pairs[p].wait_recv()
        pending.append(pairs[p])

        def one(i, carry):
            total[i] = total[i] + partner[i]
            return carry

        lax.fori_loop(p * DEPTH, (p + 1) * DEPTH, one, 0)
        first(p, 0)

    def middle(p):
        third(p, 0)
        first(p, 1)

    spread = []

    def finish(p):
        third(p, 1)
        for d in range(1, NZ):
            goal = lax.rem(z + d, NZ)

            @pl.when(lax.rem(goal, PIECES) == p)
            def _():
                pltpu.make_async_remote_copy(
                    src_ref=total.at[position(goal), y, x], dst_ref=columns.at[z],
                    send_sem=tgt_send.at[d - 1], recv_sem=tgt_recv.at[d - 1],
                    device_id={"tgt": goal}, device_id_type=MESH,
                ).start()

    begin(0)
    begin(1)
    second(0, 0)
    second(1, 0)
    begin(2)
    begin(3)
    middle(0)
    middle(1)
    second(2, 0)
    second(3, 0)
    second(0, 1)
    second(1, 1)
    middle(2)
    middle(3)
    finish(0)
    finish(1)
    second(2, 1)
    second(3, 1)
    finish(2)
    finish(3)
    columns[z] = total[position(z), y, x]
    for copy in pending:
        copy.wait_send()
    for d in range(1, NZ):
        goal = lax.rem(z + d, NZ)
        pltpu.make_async_remote_copy(
            src_ref=total.at[position(goal), y, x], dst_ref=columns.at[z],
            send_sem=tgt_send.at[d - 1], recv_sem=tgt_recv.at[d - 1],
            device_id={"tgt": goal}, device_id_type=MESH,
        ).wait()
    for tgt in range(NZ):
        for n in range(4):
            result[n, pl.ds(tgt * ROWS, ROWS), :] = columns[tgt, pl.ds(n * ROWS, ROWS), :]


def reduce(partial):
    return pl.pallas_call(
        reduce_kernel,
        out_shape=jax.ShapeDtypeStruct((4, NZ * ROWS, WIDTH), jnp.float32),
        in_specs=[pl.BlockSpec(memory_space=pl.ANY)],
        out_specs=pl.BlockSpec(memory_space=pltpu.VMEM),
        scratch_shapes=[
            pltpu.VMEM((NZ, NY, NX, 16, WIDTH), jnp.float32),
            pltpu.VMEM((NZ, NY, NX, 16, WIDTH), jnp.float32),
            pltpu.VMEM((PIECES, 6, HALF, 4, 16, WIDTH), jnp.float32),
            pltpu.VMEM((PIECES, 6, HALF, 16, WIDTH), jnp.float32),
            pltpu.VMEM((NZ, 16, WIDTH), jnp.float32),
            pltpu.SemaphoreType.DMA((PIECES,)),
            pltpu.SemaphoreType.DMA((PIECES,)),
            pltpu.SemaphoreType.DMA((PIECES,)),
            pltpu.SemaphoreType.DMA((PIECES, 2, 6)),
            pltpu.SemaphoreType.DMA((PIECES, 2, 6)),
            pltpu.SemaphoreType.DMA((NZ - 1,)),
            pltpu.SemaphoreType.DMA((NZ - 1,)),
        ],
        compiler_params=pltpu.CompilerParams(
            collective_id=1, has_side_effects=True, vmem_limit_bytes=24 * 1024 * 1024
        ),
        name="reduce",
    )(partial)


def on_device(source_coef, couplings, block_list, block_count):
    codes, blocks = exchange(block_list.reshape(3, 4, 128), block_count, couplings)
    coef = source_coef.reshape(SOURCES * ROWS, WIDTH)
    partial = apply(codes, coef, blocks)
    return reduce(partial.reshape(2, NZ, NY, NX, 16, WIDTH))


def solution(mesh):
    in_specs = (
        P("src", "tgt", None),
        P("src", None, None),
        P(None, "tgt", "src", None),
        P("tgt", "src"),
    )
    out_specs = P(("tgt", "src"), None, None)
    return jax.shard_map(
        on_device, mesh=mesh, in_specs=in_specs, out_specs=out_specs, check_vma=False
    )
```

```python
import functools

import jax
import jax.numpy as jnp
from jax import lax
from jax.experimental import pallas as pl
from jax.experimental.pallas import tpu as pltpu
from jax.sharding import PartitionSpec as P

MESH = pl.DeviceIdType.MESH
NX, NY, NZ = 4, 4, 16
PLANE = NX * NY
KINDS, COEF, WIDTH = 64, 64, 128
SOURCES, ROWS = 256, 4
TARGETS, SLOTS = 128, 512
PIECES = 4
DEPTH = NZ // PIECES
HALF = DEPTH // 2
TROWS = TARGETS * ROWS
UNROLL = 32
STRIDE = 528


def position(tgt):
    return lax.rem(tgt, PIECES) * DEPTH + tgt // PIECES


def exchange_kernel(
    lists, count, own, coef, codes, images_low, images_high, blocks, packed, spread, inputs,
    plane_send, plane_recv, core_send, core_recv, tgt_send, tgt_recv, local_sem,
):
    z, s = lax.axis_index("tgt"), lax.axis_index("src")
    core, chip = lax.rem(s, 2), s // 2
    x, y = lax.rem(chip, NX), chip // NX
    other = s + 1 - 2 * core

    def chip_at(n, sign):
        dx, dy = sign * (n % NX), sign * (n // NX)
        return lax.rem(y + dy + NY, NY) * NX + lax.rem(x + dx + NX, NX)

    barrier = pltpu.get_barrier_semaphore()
    peers = [{"src": other}]
    peers += [{"src": 2 * chip_at(n, 1) + core} for n in range(1, PLANE)]
    peers += [{"tgt": lax.rem(z + d, NZ)} for d in range(1, NZ)]
    for peer in peers:
        pl.semaphore_signal(barrier, inc=1, device_id=peer, device_id_type=MESH)

    usable = count[0, 0]
    place = (
        lax.broadcasted_iota(jnp.int32, (4, 128), 0) * 128
        + lax.broadcasted_iota(jnp.int32, (4, 128), 1)
    )
    packed[pl.ds(0, 4), :] = lists[2] * STRIDE + lists[1] * 2
    packed[pl.ds(4, 4), :] = (
        jnp.where(place < usable, lists[0] * ROWS, TROWS)
        + jnp.where(place == 0, usable * 1024, 0)
    )
    keep_blocks = pltpu.make_async_copy(own, blocks.at[pl.ds(2 * s, 2)], local_sem.at[0])
    keep_blocks.start()
    keep_codes = pltpu.make_async_copy(packed, codes.at[z], local_sem.at[1])
    keep_codes.start()

    spread[0] = coef[...].astype(jnp.float32)
    spread[1] = jnp.zeros_like(spread[1])
    spread[2] = jnp.zeros_like(spread[2])
    for row in range(ROWS):
        half = row // 2
        spread[1 + half, pl.ds(row, SOURCES, stride=2), :] = spread[
            0, pl.ds(row, SOURCES, stride=ROWS), :
        ]
        if row % 2 == 1:
            inputs[half] = spread[1 + half, pl.ds(0, STRIDE), :].astype(jnp.bfloat16)

    pl.semaphore_wait(barrier, len(peers))

    def plane_copy(n):
        return pltpu.make_async_remote_copy(
            src_ref=own, dst_ref=blocks.at[pl.ds(2 * s, 2)],
            send_sem=plane_send.at[n], recv_sem=plane_recv.at[n],
            device_id={"src": 2 * chip_at(n, 1) + core}, device_id_type=MESH,
        )

    def tgt_copy(d):
        return pltpu.make_async_remote_copy(
            src_ref=packed, dst_ref=codes.at[z],
            send_sem=tgt_send.at[d], recv_sem=tgt_recv.at[d],
            device_id={"tgt": lax.rem(z + d, NZ)}, device_id_type=MESH,
        )

    def core_copy(n):
        owner = pl.ds(4 * chip_at(n, -1) + 2 * core, 2)
        return pltpu.make_async_remote_copy(
            src_ref=blocks.at[owner], dst_ref=blocks.at[owner],
            send_sem=core_send.at[n], recv_sem=core_recv.at[n],
            device_id={"src": other}, device_id_type=MESH,
        )

    for n in range(1, PLANE):
        plane_copy(n).start()
    keep_blocks.wait()
    core_copy(0).start()
    for d in range(1, NZ):
        tgt_copy(d).start()

    sign = jnp.where(
        lax.broadcasted_iota(jnp.int32, (COEF, WIDTH), 1) < COEF, -1.0, 1.0
    ).astype(jnp.float32)

    def square(kind):
        upper = blocks[kind]
        turned = pltpu.roll(upper.astype(jnp.float32), COEF, 1) * sign
        return jnp.concatenate([upper, turned.astype(jnp.bfloat16)], axis=0)

    def build(kinds):
        wide = jnp.concatenate([square(kind) for kind in kinds], axis=1)
        for half, images in enumerate((images_low, images_high)):
            product = jnp.dot(inputs[half], wide, preferred_element_type=jnp.float32)
            for n, kind in enumerate(kinds):
                rows = pl.ds(pl.multiple_of(kind * STRIDE, STRIDE), STRIDE)
                images[rows, :] = product[:, n * WIDTH:(n + 1) * WIDTH]

    def pair(n, which):
        first = 4 * chip_at(n, -1) + 2 * which
        return [first, first + 1]

    build(pair(0, core))

    def step(n, carry):
        plane_copy(n).wait_recv()
        core_copy(n).start()
        core_copy(n - 1).wait_recv()
        build(pair(n, core) + pair(n - 1, 1 - core))
        return carry

    lax.fori_loop(1, PLANE, step, 0)
    core_copy(PLANE - 1).wait_recv()
    build(pair(PLANE - 1, 1 - core))
    for d in range(1, NZ):
        tgt_copy(d).wait()
    for n in range(PLANE):
        core_copy(n).wait_send()
    for n in range(1, PLANE):
        plane_copy(n).wait_send()
    keep_codes.wait()


def exchange(lists, count, couplings, coef):
    vmem = pl.BlockSpec(memory_space=pltpu.VMEM)
    return pl.pallas_call(
        exchange_kernel,
        out_shape=[
            pltpu.VMEM((NZ, 8, 128), jnp.int32),
            pltpu.VMEM((KINDS * STRIDE, WIDTH), jnp.float32),
            pltpu.VMEM((KINDS * STRIDE, WIDTH), jnp.float32),
        ],
        in_specs=[vmem, pl.BlockSpec(memory_space=pltpu.SMEM), vmem, vmem],
        out_specs=[vmem, vmem, vmem],
        scratch_shapes=[
            pltpu.VMEM((KINDS, COEF, WIDTH), jnp.bfloat16),
            pltpu.VMEM((8, 128), jnp.int32),
            pltpu.VMEM((3, SOURCES * ROWS, WIDTH), jnp.float32),
            pltpu.VMEM((2, STRIDE, WIDTH), jnp.bfloat16),
            pltpu.SemaphoreType.DMA((PLANE,)),
            pltpu.SemaphoreType.DMA((PLANE,)),
            pltpu.SemaphoreType.DMA((PLANE,)),
            pltpu.SemaphoreType.DMA((PLANE,)),
            pltpu.SemaphoreType.DMA((NZ,)),
            pltpu.SemaphoreType.DMA((NZ,)),
            pltpu.SemaphoreType.DMA((2,)),
        ],
        compiler_params=pltpu.CompilerParams(
            collective_id=0, has_side_effects=True, vmem_limit_bytes=8 * 1024 * 1024
        ),
        name="exchange",
    )(lists, count, couplings, coef)


def apply_kernel(codes, images_low, images_high, out, *totals):
    low = lax.broadcasted_iota(jnp.int32, (ROWS, WIDTH), 0) < 2

    def add_list(tgt, carry):
        for total in totals:
            total[...] = jnp.zeros_like(total)
        base = tgt * 1024
        used = lax.shift_right_logical(codes[base + SLOTS], 10)

        def add_group(group, carry):
            start = base + group * UNROLL
            for n in range(UNROLL):
                image, target = codes[start + n], codes[start + SLOTS + n]
                if n == 0:
                    target = jnp.bitwise_and(target, 1023)
                value = jnp.where(
                    low, images_low[pl.ds(image, ROWS), :], images_high[pl.ds(image, ROWS), :]
                )
                totals[n % len(totals)][pl.ds(target, ROWS), :] += value
            return carry

        lax.fori_loop(0, (used + UNROLL - 1) // UNROLL, add_group, 0)
        for chip in range(PLANE):
            for core in range(2):
                rows = pl.ds((2 * chip + core) * 16, 16)
                value = totals[0][rows, :]
                for total in totals[1:]:
                    value = value + total[rows, :]
                out[core, position(tgt), chip] = value
        return carry

    lax.fori_loop(0, NZ, add_list, 0)


def apply(codes, images_low, images_high):
    return pl.pallas_call(
        apply_kernel,
        out_shape=pltpu.VMEM((2, NZ, PLANE, 16, WIDTH), jnp.float32),
        in_specs=[
            pl.BlockSpec(memory_space=pltpu.SMEM),
            pl.BlockSpec(memory_space=pltpu.VMEM),
            pl.BlockSpec(memory_space=pltpu.VMEM),
        ],
        out_specs=pl.BlockSpec(memory_space=pltpu.VMEM),
        scratch_shapes=[pltpu.VMEM((TROWS + 8, WIDTH), jnp.float32)] * 4,
        compiler_params=pltpu.CompilerParams(vmem_limit_bytes=4 * 1024 * 1024),
        name="apply",
    )(codes, images_low, images_high)


def reduce_kernel(
    partial, result, total, partner, wide, narrow, columns,
    local_sem, pair_send, pair_recv, ring_send, ring_recv, tgt_send, tgt_recv,
):
    z, s = lax.axis_index("tgt"), lax.axis_index("src")
    core, chip = lax.rem(s, 2), s // 2
    x, y = lax.rem(chip, NX), chip // NX
    other = s + 1 - 2 * core

    def device(cy, cx):
        return {"src": (lax.rem(cy, NY) * NX + lax.rem(cx, NX)) * 2 + core}

    ahead = (device(y, x + 1), device(y + 1, x))
    behind = (device(y, x + NX - 1), device(y + NY - 1, x))
    barrier = pltpu.get_barrier_semaphore()
    peers = [{"src": other}, *ahead, *behind]
    peers += [{"tgt": lax.rem(z + d, NZ)} for d in range(1, NZ)]
    for peer in peers:
        pl.semaphore_signal(barrier, inc=1, device_id=peer, device_id_type=MESH)

    mine = []
    for p in range(PIECES):
        span = pl.ds(p * DEPTH, DEPTH)
        mine.append(pltpu.make_async_copy(
            partial.at[core, span], total.at[span], local_sem.at[p]))
        mine[-1].start()
    pl.semaphore_wait(barrier, len(peers))
    pairs = []
    for p in range(PIECES):
        span = pl.ds(p * DEPTH, DEPTH)
        pairs.append(pltpu.make_async_remote_copy(
            src_ref=partial.at[1 - core, span], dst_ref=partner.at[span],
            send_sem=pair_send.at[p], recv_sem=pair_recv.at[p],
            device_id={"src": other}, device_id_type=MESH,
        ))
        pairs[-1].start()

    here = (x, y)
    pending = []

    def cut(p, level, index, part):
        axis = (p + level) % 2
        span = pl.ds(p * DEPTH + part * HALF, HALF)
        if level == 0:
            return total.at[span, :, index] if axis == 0 else total.at[span, index]
        return total.at[span, index, x] if axis == 1 else total.at[span, y, index]

    def slot(p, level, n):
        return wide.at[p, n] if level == 0 else narrow.at[p, n]

    def send(p, level, n, ref):
        axis = (p + level) % 2
        copy = pltpu.make_async_remote_copy(
            src_ref=ref, dst_ref=slot(p, level, n),
            send_sem=ring_send.at[p, level, n], recv_sem=ring_recv.at[p, level, n],
            device_id=(ahead if n % 2 == 0 else behind)[axis], device_id_type=MESH,
        )
        copy.start()
        pending.append(copy)
        return copy

    rings = {}

    def add(ref, *others):
        value = ref[...]
        for one in others:
            value = value + one[...]
        ref[...] = value

    def first(p, level):
        me = here[(p + level) % 2]
        up, far, down = lax.rem(me + 1, 4), lax.rem(me + 2, 4), lax.rem(me + 3, 4)
        ring = {}
        ring[0] = send(p, level, 0, cut(p, level, far, 0))
        ring[1] = send(p, level, 1, cut(p, level, far, 1))
        ring[2] = send(p, level, 2, cut(p, level, up, 1))
        ring[3] = send(p, level, 3, cut(p, level, down, 0))
        rings[p, level] = ring

    def second(p, level):
        me = here[(p + level) % 2]
        up, down = lax.rem(me + 1, 4), lax.rem(me + 3, 4)
        ring = rings[p, level]
        ring[0].wait_recv()
        add(cut(p, level, up, 0), slot(p, level, 0))
        ring[4] = send(p, level, 4, cut(p, level, up, 0))
        ring[1].wait_recv()
        add(cut(p, level, down, 1), slot(p, level, 1))
        ring[5] = send(p, level, 5, cut(p, level, down, 1))

    def third(p, level):
        me = here[(p + level) % 2]
        ring = rings[p, level]
        for n in (2, 3, 4, 5):
            ring[n].wait_recv()
        add(cut(p, level, me, 0), slot(p, level, 3), slot(p, level, 4))
        add(cut(p, level, me, 1), slot(p, level, 2), slot(p, level, 5))

    def begin(p):
        mine[p].wait()
        pairs[p].wait_recv()
        pending.append(pairs[p])

        def one(i, carry):
            total[i] = total[i] + partner[i]
            return carry

        lax.fori_loop(p * DEPTH, (p + 1) * DEPTH, one, 0)
        first(p, 0)

    def middle(p):
        third(p, 0)
        first(p, 1)

    spread = []

    def finish(p):
        third(p, 1)
        for d in range(1, NZ):
            goal = lax.rem(z + d, NZ)

            @pl.when(lax.rem(goal, PIECES) == p)
            def _():
                pltpu.make_async_remote_copy(
                    src_ref=total.at[position(goal), y, x], dst_ref=columns.at[z],
                    send_sem=tgt_send.at[d - 1], recv_sem=tgt_recv.at[d - 1],
                    device_id={"tgt": goal}, device_id_type=MESH,
                ).start()

    begin(0)
    begin(1)
    second(0, 0)
    second(1, 0)
    begin(2)
    begin(3)
    middle(0)
    middle(1)
    second(2, 0)
    second(3, 0)
    second(0, 1)
    second(1, 1)
    middle(2)
    middle(3)
    finish(0)
    finish(1)
    second(2, 1)
    second(3, 1)
    finish(2)
    finish(3)
    columns[z] = total[position(z), y, x]
    for copy in pending:
        copy.wait_send()
    for d in range(1, NZ):
        goal = lax.rem(z + d, NZ)
        pltpu.make_async_remote_copy(
            src_ref=total.at[position(goal), y, x], dst_ref=columns.at[z],
            send_sem=tgt_send.at[d - 1], recv_sem=tgt_recv.at[d - 1],
            device_id={"tgt": goal}, device_id_type=MESH,
        ).wait()
    for tgt in range(NZ):
        for n in range(4):
            result[n, pl.ds(tgt * ROWS, ROWS), :] = columns[tgt, pl.ds(n * ROWS, ROWS), :]


def reduce(partial):
    return pl.pallas_call(
        reduce_kernel,
        out_shape=jax.ShapeDtypeStruct((4, NZ * ROWS, WIDTH), jnp.float32),
        in_specs=[pl.BlockSpec(memory_space=pl.ANY)],
        out_specs=pl.BlockSpec(memory_space=pltpu.VMEM),
        scratch_shapes=[
            pltpu.VMEM((NZ, NY, NX, 16, WIDTH), jnp.float32),
            pltpu.VMEM((NZ, NY, NX, 16, WIDTH), jnp.float32),
            pltpu.VMEM((PIECES, 6, HALF, 4, 16, WIDTH), jnp.float32),
            pltpu.VMEM((PIECES, 6, HALF, 16, WIDTH), jnp.float32),
            pltpu.VMEM((NZ, 16, WIDTH), jnp.float32),
            pltpu.SemaphoreType.DMA((PIECES,)),
            pltpu.SemaphoreType.DMA((PIECES,)),
            pltpu.SemaphoreType.DMA((PIECES,)),
            pltpu.SemaphoreType.DMA((PIECES, 2, 6)),
            pltpu.SemaphoreType.DMA((PIECES, 2, 6)),
            pltpu.SemaphoreType.DMA((NZ - 1,)),
            pltpu.SemaphoreType.DMA((NZ - 1,)),
        ],
        compiler_params=pltpu.CompilerParams(
            collective_id=1, has_side_effects=True, vmem_limit_bytes=12 * 1024 * 1024
        ),
        name="reduce",
    )(partial)


def on_device(source_coef, couplings, block_list, block_count):
    coef = source_coef.reshape(SOURCES * ROWS, WIDTH)
    codes, low, high = exchange(block_list.reshape(3, 4, 128), block_count, couplings, coef)
    partial = apply(codes.reshape(NZ * 1024), low, high)
    return reduce(partial.reshape(2, NZ, NY, NX, 16, WIDTH))


def solution(mesh):
    in_specs = (
        P("src", "tgt", None),
        P("src", None, None),
        P(None, "tgt", "src", None),
        P("tgt", "src"),
    )
    out_specs = P(("tgt", "src"), None, None)
    return jax.shard_map(
        on_device, mesh=mesh, in_specs=in_specs, out_specs=out_specs, check_vma=False
    )
```

```python
import functools

import jax
import jax.numpy as jnp
from jax import lax
from jax.experimental import pallas as pl
from jax.experimental.pallas import tpu as pltpu
from jax.sharding import PartitionSpec as P

MESH = pl.DeviceIdType.MESH
NX, NY, NZ = 4, 4, 16
PLANE = NX * NY
KINDS, COEF, WIDTH = 64, 64, 128
SOURCES, ROWS = 256, 4
TARGETS, SLOTS = 128, 512
PIECES = 8
DEPTH = NZ // PIECES
HALF = DEPTH // 2
TROWS = TARGETS * ROWS
UNROLL = 32
STRIDE = 528
NEAREST = (0, 1, 3, 4, 12, 2, 8, 5, 13, 7, 15, 6, 14, 9, 11, 10)


def position(tgt):
    return (tgt % PIECES) * DEPTH + tgt // PIECES


def exchange_kernel(
    lists_in, count, own, coef_in, codes, images_low, images_high, blocks, packed, spread, inputs,
    lists, coef,
    plane_send, plane_recv, core_send, core_recv, tgt_send, tgt_recv, local_sem,
):
    z, s = lax.axis_index("tgt"), lax.axis_index("src")
    core, chip = lax.rem(s, 2), s // 2
    x, y = lax.rem(chip, NX), chip // NX
    other = s + 1 - 2 * core

    def chip_at(n, sign):
        if isinstance(n, int):
            shift = NEAREST[n]
        else:
            shift = sum(jnp.where(n == m, NEAREST[m], 0) for m in range(1, PLANE))
        dx, dy = sign * (shift % NX), sign * (shift // NX)
        return lax.rem(y + dy + NY, NY) * NX + lax.rem(x + dx + NX, NX)

    load_lists = pltpu.make_async_copy(lists_in, lists, local_sem.at[2])
    load_lists.start()
    keep_blocks = pltpu.make_async_copy(own, blocks.at[pl.ds(2 * s, 2)], local_sem.at[0])
    keep_blocks.start()
    load_coef = pltpu.make_async_copy(coef_in, coef, local_sem.at[3])
    load_coef.start()
    barrier = pltpu.get_barrier_semaphore()
    peers = [{"src": other}]
    peers += [{"src": 2 * chip_at(n, 1) + core} for n in range(1, PLANE)]
    peers += [{"tgt": lax.rem(z + d, NZ)} for d in range(1, NZ)]
    for peer in peers:
        pl.semaphore_signal(barrier, inc=1, device_id=peer, device_id_type=MESH)

    usable = count[0, 0]
    place = (
        lax.broadcasted_iota(jnp.int32, (4, 128), 0) * 128
        + lax.broadcasted_iota(jnp.int32, (4, 128), 1)
    )
    load_lists.wait()
    packed[pl.ds(0, 4), :] = lists[2] * STRIDE + lists[1] * 2
    packed[pl.ds(4, 4), :] = (
        jnp.where(place < usable, lists[0] * ROWS, TROWS)
        + jnp.where(place == 0, usable * 1024, 0)
    )
    keep_codes = pltpu.make_async_copy(packed, codes.at[z], local_sem.at[1])
    keep_codes.start()

    load_coef.wait()
    spread[0] = coef[...].astype(jnp.float32)
    spread[1] = jnp.zeros_like(spread[1])
    spread[2] = jnp.zeros_like(spread[2])
    for row in range(ROWS):
        half = row // 2
        spread[1 + half, pl.ds(row, SOURCES, stride=2), :] = spread[
            0, pl.ds(row, SOURCES, stride=ROWS), :
        ]
        if row % 2 == 1:
            inputs[half] = spread[1 + half, pl.ds(0, STRIDE), :].astype(jnp.bfloat16)

    pl.semaphore_wait(barrier, len(peers))

    def plane_copy(n):
        return pltpu.make_async_remote_copy(
            src_ref=own, dst_ref=blocks.at[pl.ds(2 * s, 2)],
            send_sem=plane_send.at[n], recv_sem=plane_recv.at[n],
            device_id={"src": 2 * chip_at(n, 1) + core}, device_id_type=MESH,
        )

    def tgt_copy(d):
        return pltpu.make_async_remote_copy(
            src_ref=packed, dst_ref=codes.at[z],
            send_sem=tgt_send.at[d], recv_sem=tgt_recv.at[d],
            device_id={"tgt": lax.rem(z + d, NZ)}, device_id_type=MESH,
        )

    def core_copy(n):
        owner = pl.ds(4 * chip_at(n, -1) + 2 * core, 2)
        return pltpu.make_async_remote_copy(
            src_ref=blocks.at[owner], dst_ref=blocks.at[owner],
            send_sem=core_send.at[n], recv_sem=core_recv.at[n],
            device_id={"src": other}, device_id_type=MESH,
        )

    for n in range(1, PLANE):
        plane_copy(n).start()
    keep_blocks.wait()
    core_copy(0).start()
    for d in range(1, NZ):
        tgt_copy(d).start()

    sign = jnp.where(
        lax.broadcasted_iota(jnp.int32, (COEF, WIDTH), 1) < COEF, -1.0, 1.0
    ).astype(jnp.float32)

    def square(kind):
        upper = blocks[kind]
        turned = pltpu.roll(upper.astype(jnp.float32), COEF, 1) * sign
        return jnp.concatenate([upper, turned.astype(jnp.bfloat16)], axis=0)

    def build(kinds):
        wide = jnp.concatenate([square(kind) for kind in kinds], axis=1)
        for half, images in enumerate((images_low, images_high)):
            product = jnp.dot(inputs[half], wide, preferred_element_type=jnp.float32)
            for n, kind in enumerate(kinds):
                rows = pl.ds(pl.multiple_of(kind * STRIDE, STRIDE), STRIDE)
                images[rows, :] = product[:, n * WIDTH:(n + 1) * WIDTH]

    def pair(n, which):
        first = 4 * chip_at(n, -1) + 2 * which
        return [first, first + 1]

    build(pair(0, core))

    def step(n, carry):
        plane_copy(n).wait_recv()
        core_copy(n).start()
        core_copy(n - 1).wait_recv()
        build(pair(n, core) + pair(n - 1, 1 - core))
        return carry

    lax.fori_loop(1, PLANE, step, 0)
    core_copy(PLANE - 1).wait_recv()
    build(pair(PLANE - 1, 1 - core))
    for d in range(1, NZ):
        tgt_copy(d).wait()
    for n in range(PLANE):
        core_copy(n).wait_send()
    for n in range(1, PLANE):
        plane_copy(n).wait_send()
    keep_codes.wait()


def exchange(lists, count, couplings, coef):
    vmem = pl.BlockSpec(memory_space=pltpu.VMEM)
    hbm = pl.BlockSpec(memory_space=pltpu.HBM)
    lists, couplings, coef = (
        pltpu.with_memory_space_constraint(one, pltpu.HBM) for one in (lists, couplings, coef)
    )
    return pl.pallas_call(
        exchange_kernel,
        out_shape=[
            pltpu.VMEM((NZ, 8, 128), jnp.int32),
            pltpu.VMEM((KINDS * STRIDE, WIDTH), jnp.float32),
            pltpu.VMEM((KINDS * STRIDE, WIDTH), jnp.float32),
        ],
        in_specs=[hbm, pl.BlockSpec(memory_space=pltpu.SMEM), hbm, hbm],
        out_specs=[vmem, vmem, vmem],
        scratch_shapes=[
            pltpu.VMEM((KINDS, COEF, WIDTH), jnp.bfloat16),
            pltpu.VMEM((8, 128), jnp.int32),
            pltpu.VMEM((3, SOURCES * ROWS, WIDTH), jnp.float32),
            pltpu.VMEM((2, STRIDE, WIDTH), jnp.bfloat16),
            pltpu.VMEM((3, 4, 128), jnp.int32),
            pltpu.VMEM((SOURCES * ROWS, WIDTH), jnp.bfloat16),
            pltpu.SemaphoreType.DMA((PLANE,)),
            pltpu.SemaphoreType.DMA((PLANE,)),
            pltpu.SemaphoreType.DMA((PLANE,)),
            pltpu.SemaphoreType.DMA((PLANE,)),
            pltpu.SemaphoreType.DMA((NZ,)),
            pltpu.SemaphoreType.DMA((NZ,)),
            pltpu.SemaphoreType.DMA((4,)),
        ],
        compiler_params=pltpu.CompilerParams(
            collective_id=0, has_side_effects=True, vmem_limit_bytes=8 * 1024 * 1024
        ),
        name="exchange",
    )(lists, count, couplings, coef)


def apply_kernel(codes, images_low, images_high, out, *totals):
    low = lax.broadcasted_iota(jnp.int32, (ROWS, WIDTH), 0) < 2

    def add_list(tgt, carry):
        for total in totals:
            total[...] = jnp.zeros_like(total)
        base = tgt * 1024
        used = lax.shift_right_logical(codes[base + SLOTS], 10)

        def add_group(group, carry):
            start = base + group * UNROLL
            for n in range(UNROLL):
                image, target = codes[start + n], codes[start + SLOTS + n]
                if n == 0:
                    target = jnp.bitwise_and(target, 1023)
                value = jnp.where(
                    low, images_low[pl.ds(image, ROWS), :], images_high[pl.ds(image, ROWS), :]
                )
                totals[n % len(totals)][pl.ds(target, ROWS), :] += value
            return carry

        lax.fori_loop(0, (used + UNROLL - 1) // UNROLL, add_group, 0)
        for chip in range(PLANE):
            for core in range(2):
                rows = pl.ds((2 * chip + core) * 16, 16)
                value = totals[0][rows, :]
                for total in totals[1:]:
                    value = value + total[rows, :]
                out[core, position(tgt), chip] = value
        return carry

    lax.fori_loop(0, NZ, add_list, 0)


def apply(codes, images_low, images_high):
    return pl.pallas_call(
        apply_kernel,
        out_shape=pltpu.VMEM((2, NZ, PLANE, 16, WIDTH), jnp.float32),
        in_specs=[
            pl.BlockSpec(memory_space=pltpu.SMEM),
            pl.BlockSpec(memory_space=pltpu.VMEM),
            pl.BlockSpec(memory_space=pltpu.VMEM),
        ],
        out_specs=pl.BlockSpec(memory_space=pltpu.VMEM),
        scratch_shapes=[pltpu.VMEM((TROWS + 8, WIDTH), jnp.float32)] * 4,
        compiler_params=pltpu.CompilerParams(vmem_limit_bytes=4 * 1024 * 1024),
        name="apply",
    )(codes, images_low, images_high)


def reduce_kernel(
    partial, result, total, partner, wide, narrow, columns,
    local_sem, pair_send, pair_recv, ring_send, ring_recv, tgt_send, tgt_recv,
):
    z, s = lax.axis_index("tgt"), lax.axis_index("src")
    core, chip = lax.rem(s, 2), s // 2
    x, y = lax.rem(chip, NX), chip // NX
    other = s + 1 - 2 * core

    def device(cy, cx):
        return {"src": (lax.rem(cy, NY) * NX + lax.rem(cx, NX)) * 2 + core}

    ahead = (device(y, x + 1), device(y + 1, x))
    behind = (device(y, x + NX - 1), device(y + NY - 1, x))
    barrier = pltpu.get_barrier_semaphore()
    peers = [{"src": other}, *ahead, *behind]
    peers += [{"tgt": lax.rem(z + d, NZ)} for d in range(1, NZ)]
    for peer in peers:
        pl.semaphore_signal(barrier, inc=1, device_id=peer, device_id_type=MESH)

    mine = []
    for p in range(PIECES):
        span = pl.ds(p * DEPTH, DEPTH)
        mine.append(pltpu.make_async_copy(
            partial.at[core, span], total.at[span], local_sem.at[p]))
        mine[-1].start()
    pl.semaphore_wait(barrier, len(peers))
    pairs = []
    for p in range(PIECES):
        span = pl.ds(p * DEPTH, DEPTH)
        pairs.append(pltpu.make_async_remote_copy(
            src_ref=partial.at[1 - core, span], dst_ref=partner.at[span],
            send_sem=pair_send.at[p], recv_sem=pair_recv.at[p],
            device_id={"src": other}, device_id_type=MESH,
        ))
        pairs[-1].start()

    here = (x, y)
    pending = []

    def cut(p, level, index, part):
        axis = (p + level) % 2
        span = pl.ds(p * DEPTH + part * HALF, HALF)
        if level == 0:
            return total.at[span, :, index] if axis == 0 else total.at[span, index]
        return total.at[span, index, x] if axis == 1 else total.at[span, y, index]

    def slot(p, level, n):
        return wide.at[p, n] if level == 0 else narrow.at[p, n]

    def send(p, level, n, ref):
        axis = (p + level) % 2
        copy = pltpu.make_async_remote_copy(
            src_ref=ref, dst_ref=slot(p, level, n),
            send_sem=ring_send.at[p, level, n], recv_sem=ring_recv.at[p, level, n],
            device_id=(ahead if n % 2 == 0 else behind)[axis], device_id_type=MESH,
        )
        copy.start()
        pending.append(copy)
        return copy

    rings = {}

    def add(ref, *others):
        value = ref[...]
        for one in others:
            value = value + one[...]
        ref[...] = value

    def first(p, level):
        me = here[(p + level) % 2]
        up, far, down = lax.rem(me + 1, 4), lax.rem(me + 2, 4), lax.rem(me + 3, 4)
        ring = {}
        ring[0] = send(p, level, 0, cut(p, level, far, 0))
        ring[1] = send(p, level, 1, cut(p, level, far, 1))
        ring[2] = send(p, level, 2, cut(p, level, up, 1))
        ring[3] = send(p, level, 3, cut(p, level, down, 0))
        rings[p, level] = ring

    def second(p, level):
        me = here[(p + level) % 2]
        up, down = lax.rem(me + 1, 4), lax.rem(me + 3, 4)
        ring = rings[p, level]
        ring[0].wait_recv()
        add(cut(p, level, up, 0), slot(p, level, 0))
        ring[4] = send(p, level, 4, cut(p, level, up, 0))
        ring[1].wait_recv()
        add(cut(p, level, down, 1), slot(p, level, 1))
        ring[5] = send(p, level, 5, cut(p, level, down, 1))

    def third(p, level):
        me = here[(p + level) % 2]
        ring = rings[p, level]
        for n in (2, 3, 4, 5):
            ring[n].wait_recv()
        add(cut(p, level, me, 0), slot(p, level, 3), slot(p, level, 4))
        add(cut(p, level, me, 1), slot(p, level, 2), slot(p, level, 5))

    def begin(p):
        mine[p].wait()
        pairs[p].wait_recv()
        pending.append(pairs[p])

        def one(i, carry):
            total[i] = total[i] + partner[i]
            return carry

        lax.fori_loop(p * DEPTH, (p + 1) * DEPTH, one, 0)
        first(p, 0)

    def middle(p):
        third(p, 0)
        first(p, 1)

    def finish(p):
        third(p, 1)
        for n in range(DEPTH):
            goal = p + n * PIECES

            @pl.when(goal != z)
            def _():
                tgt_copy(goal).start()

    def tgt_copy(goal):
        shift = lax.rem(goal - z + NZ, NZ) - 1
        return pltpu.make_async_remote_copy(
            src_ref=total.at[position(goal), y, x], dst_ref=columns.at[z],
            send_sem=tgt_send.at[shift], recv_sem=tgt_recv.at[shift],
            device_id={"tgt": goal}, device_id_type=MESH,
        )

    stages = (begin, lambda p: second(p, 0), middle, lambda p: second(p, 1), finish)
    for tick in range(PIECES // 2 + len(stages) - 1):
        for delay, stage in enumerate(stages):
            if 0 <= tick - delay < PIECES // 2:
                stage(2 * (tick - delay))
                stage(2 * (tick - delay) + 1)
    columns[z] = total[position(z), y, x]
    for copy in pending:
        copy.wait_send()
    for d in range(1, NZ):
        tgt_copy(lax.rem(z + d, NZ)).wait()
    for tgt in range(NZ):
        for n in range(4):
            result[n, pl.ds(tgt * ROWS, ROWS), :] = columns[tgt, pl.ds(n * ROWS, ROWS), :]


def reduce(partial):
    return pl.pallas_call(
        reduce_kernel,
        out_shape=jax.ShapeDtypeStruct((4, NZ * ROWS, WIDTH), jnp.float32),
        in_specs=[pl.BlockSpec(memory_space=pl.ANY)],
        out_specs=pl.BlockSpec(memory_space=pltpu.VMEM),
        scratch_shapes=[
            pltpu.VMEM((NZ, NY, NX, 16, WIDTH), jnp.float32),
            pltpu.VMEM((NZ, NY, NX, 16, WIDTH), jnp.float32),
            pltpu.VMEM((PIECES, 6, HALF, 4, 16, WIDTH), jnp.float32),
            pltpu.VMEM((PIECES, 6, HALF, 16, WIDTH), jnp.float32),
            pltpu.VMEM((NZ, 16, WIDTH), jnp.float32),
            pltpu.SemaphoreType.DMA((PIECES,)),
            pltpu.SemaphoreType.DMA((PIECES,)),
            pltpu.SemaphoreType.DMA((PIECES,)),
            pltpu.SemaphoreType.DMA((PIECES, 2, 6)),
            pltpu.SemaphoreType.DMA((PIECES, 2, 6)),
            pltpu.SemaphoreType.DMA((NZ - 1,)),
            pltpu.SemaphoreType.DMA((NZ - 1,)),
        ],
        compiler_params=pltpu.CompilerParams(
            collective_id=1, has_side_effects=True, vmem_limit_bytes=12 * 1024 * 1024
        ),
        name="reduce",
    )(partial)


def on_device(source_coef, couplings, block_list, block_count):
    coef = source_coef.reshape(SOURCES * ROWS, WIDTH)
    codes, low, high = exchange(block_list.reshape(3, 4, 128), block_count, couplings, coef)
    partial = apply(codes.reshape(NZ * 1024), low, high)
    return reduce(partial.reshape(2, NZ, NY, NX, 16, WIDTH))


def solution(mesh):
    in_specs = (
        P("src", "tgt", None),
        P("src", None, None),
        P(None, "tgt", "src", None),
        P("tgt", "src"),
    )
    out_specs = P(("tgt", "src"), None, None)
    return jax.shard_map(
        on_device, mesh=mesh, in_specs=in_specs, out_specs=out_specs, check_vma=False
    )
```

```python
import functools

import jax
import jax.numpy as jnp
from jax import lax
from jax.experimental import pallas as pl
from jax.experimental.pallas import tpu as pltpu
from jax.sharding import PartitionSpec as P

MESH = pl.DeviceIdType.MESH
NX, NY, NZ = 4, 4, 16
PLANE = NX * NY
KINDS, COEF, WIDTH = 64, 64, 128
SOURCES, ROWS = 256, 4
TARGETS, SLOTS = 128, 512
PIECES = 8
DEPTH = NZ // PIECES
HALF = DEPTH // 2
TROWS = TARGETS * ROWS
UNROLL = 32
STRIDE = 528
GROUP = 2
NEAREST = (0, 1, 3, 4, 12, 2, 8, 5, 13, 7, 15, 6, 14, 9, 11, 10)


def position(tgt):
    return (tgt % PIECES) * DEPTH + tgt // PIECES


def exchange_kernel(
    lists_in, count, own, coef_in, codes, images_low, images_high, blocks, packed, spread, inputs,
    lists, coef,
    plane_send, plane_recv, core_send, core_recv, tgt_send, tgt_recv, local_sem,
):
    z, s = lax.axis_index("tgt"), lax.axis_index("src")
    core, chip = lax.rem(s, 2), s // 2
    x, y = lax.rem(chip, NX), chip // NX
    other = s + 1 - 2 * core

    def chip_at(n, sign):
        if isinstance(n, int):
            shift = NEAREST[n]
        else:
            shift = sum(jnp.where(n == m, NEAREST[m], 0) for m in range(1, PLANE))
        dx, dy = sign * (shift % NX), sign * (shift // NX)
        return lax.rem(y + dy + NY, NY) * NX + lax.rem(x + dx + NX, NX)

    load_lists = pltpu.make_async_copy(lists_in, lists, local_sem.at[2])
    load_lists.start()
    keep_blocks = pltpu.make_async_copy(own, blocks.at[pl.ds(2 * s, 2)], local_sem.at[0])
    keep_blocks.start()
    load_coef = pltpu.make_async_copy(coef_in, coef, local_sem.at[3])
    load_coef.start()
    barrier = pltpu.get_barrier_semaphore()
    peers = [{"src": other}]
    peers += [{"src": 2 * chip_at(n, 1) + core} for n in range(1, PLANE)]
    peers += [{"tgt": lax.rem(z + d, NZ)} for d in range(1, NZ)]
    for peer in peers:
        pl.semaphore_signal(barrier, inc=1, device_id=peer, device_id_type=MESH)

    pl.semaphore_wait(barrier, len(peers))

    def plane_copy(n):
        return pltpu.make_async_remote_copy(
            src_ref=own, dst_ref=blocks.at[pl.ds(2 * s, 2)],
            send_sem=plane_send.at[n], recv_sem=plane_recv.at[n],
            device_id={"src": 2 * chip_at(n, 1) + core}, device_id_type=MESH,
        )

    def tgt_copy(d):
        return pltpu.make_async_remote_copy(
            src_ref=packed, dst_ref=codes.at[z],
            send_sem=tgt_send.at[d], recv_sem=tgt_recv.at[d],
            device_id={"tgt": lax.rem(z + d, NZ)}, device_id_type=MESH,
        )

    def core_copy(n):
        owner = pl.ds(4 * chip_at(n, -1) + 2 * core, 2)
        return pltpu.make_async_remote_copy(
            src_ref=blocks.at[owner], dst_ref=blocks.at[owner],
            send_sem=core_send.at[n], recv_sem=core_recv.at[n],
            device_id={"src": other}, device_id_type=MESH,
        )

    for n in range(1, PLANE):
        plane_copy(n).start()
    keep_blocks.wait()
    core_copy(0).start()

    usable = count[0, 0]
    place = (
        lax.broadcasted_iota(jnp.int32, (4, 128), 0) * 128
        + lax.broadcasted_iota(jnp.int32, (4, 128), 1)
    )
    load_lists.wait()
    packed[pl.ds(0, 4), :] = lists[2] * STRIDE + lists[1] * 2
    packed[pl.ds(4, 4), :] = (
        jnp.where(place < usable, lists[0] * ROWS, TROWS)
        + jnp.where(place == 0, usable * 1024, 0)
    )
    keep_codes = pltpu.make_async_copy(packed, codes.at[z], local_sem.at[1])
    keep_codes.start()

    for d in range(1, NZ):
        tgt_copy(d).start()

    load_coef.wait()
    spread[0] = coef[...].astype(jnp.float32)
    spread[1] = jnp.zeros_like(spread[1])
    spread[2] = jnp.zeros_like(spread[2])
    for row in range(ROWS):
        half = row // 2
        spread[1 + half, pl.ds(row, SOURCES, stride=2), :] = spread[
            0, pl.ds(row, SOURCES, stride=ROWS), :
        ]
        if row % 2 == 1:
            inputs[pl.ds(half * STRIDE, STRIDE), :] = (
                spread[1 + half, pl.ds(0, STRIDE), :].astype(jnp.bfloat16))


    sign = jnp.where(
        lax.broadcasted_iota(jnp.int32, (COEF, WIDTH), 1) < COEF, -1.0, 1.0
    ).astype(jnp.float32)

    def square(kind):
        upper = blocks[kind]
        turned = pltpu.roll(upper.astype(jnp.float32), COEF, 1) * sign
        return jnp.concatenate([upper, turned.astype(jnp.bfloat16)], axis=0)

    def build(kinds):
        wide = jnp.concatenate([square(kind) for kind in kinds], axis=1)
        for half, images in enumerate((images_low, images_high)):
            product = jnp.dot(
                inputs[pl.ds(half * STRIDE, STRIDE), :], wide,
                preferred_element_type=jnp.float32,
            )
            for n, kind in enumerate(kinds):
                rows = pl.ds(pl.multiple_of(kind * STRIDE, STRIDE), STRIDE)
                images[rows, :] = product[:, n * WIDTH:(n + 1) * WIDTH]

    def arrive(n):
        if not isinstance(n, int) or n > 0:
            plane_copy(n).wait_recv()
            core_copy(n).start()

    def step(first, own_part, other_part):
        kinds = []
        if own_part:
            for n in range(GROUP):
                arrive(first + n)
                kinds += [4 * chip_at(first + n, -1) + 2 * core + m for m in range(2)]
        if other_part:
            for n in range(GROUP):
                place = first - GROUP + n
                core_copy(place).wait_recv()
                kinds += [4 * chip_at(place, -1) + 2 * (1 - core) + m for m in range(2)]
        build(kinds)

    def both(group, carry):
        step(group * GROUP, True, True)
        return carry

    step(0, True, False)
    lax.fori_loop(1, PLANE // GROUP, both, 0)
    step(PLANE, False, True)
    for d in range(1, NZ):
        tgt_copy(d).wait()
    for n in range(PLANE):
        core_copy(n).wait_send()
    for n in range(1, PLANE):
        plane_copy(n).wait_send()
    keep_codes.wait()


def exchange(lists, count, couplings, coef):
    vmem = pl.BlockSpec(memory_space=pltpu.VMEM)
    hbm = pl.BlockSpec(memory_space=pltpu.HBM)
    lists, couplings, coef = (
        pltpu.with_memory_space_constraint(one, pltpu.HBM) for one in (lists, couplings, coef)
    )
    return pl.pallas_call(
        exchange_kernel,
        out_shape=[
            pltpu.VMEM((NZ, 8, 128), jnp.int32),
            pltpu.VMEM((KINDS * STRIDE, WIDTH), jnp.float32),
            pltpu.VMEM((KINDS * STRIDE, WIDTH), jnp.float32),
        ],
        in_specs=[hbm, pl.BlockSpec(memory_space=pltpu.SMEM), hbm, hbm],
        out_specs=[vmem, vmem, vmem],
        scratch_shapes=[
            pltpu.VMEM((KINDS, COEF, WIDTH), jnp.bfloat16),
            pltpu.VMEM((8, 128), jnp.int32),
            pltpu.VMEM((3, SOURCES * ROWS, WIDTH), jnp.float32),
            pltpu.VMEM((2 * STRIDE, WIDTH), jnp.bfloat16),
            pltpu.VMEM((3, 4, 128), jnp.int32),
            pltpu.VMEM((SOURCES * ROWS, WIDTH), jnp.bfloat16),
            pltpu.SemaphoreType.DMA((PLANE,)),
            pltpu.SemaphoreType.DMA((PLANE,)),
            pltpu.SemaphoreType.DMA((PLANE,)),
            pltpu.SemaphoreType.DMA((PLANE,)),
            pltpu.SemaphoreType.DMA((NZ,)),
            pltpu.SemaphoreType.DMA((NZ,)),
            pltpu.SemaphoreType.DMA((4,)),
        ],
        compiler_params=pltpu.CompilerParams(
            collective_id=0, has_side_effects=True, vmem_limit_bytes=14 * 1024 * 1024
        ),
        name="exchange",
    )(lists, count, couplings, coef)


def apply_kernel(codes, images_low, images_high, out, *totals):
    low = lax.broadcasted_iota(jnp.int32, (ROWS, WIDTH), 0) < 2

    for total in totals:
        total[...] = jnp.zeros_like(total)

    def add_list(tgt, carry):
        base = tgt * 1024
        used = lax.shift_right_logical(codes[base + SLOTS], 10)

        def add_group(group, carry):
            start = base + group * UNROLL
            for n in range(UNROLL):
                image, target = codes[start + n], codes[start + SLOTS + n]
                if n == 0:
                    target = jnp.bitwise_and(target, 1023)
                value = jnp.where(
                    low, images_low[pl.ds(image, ROWS), :], images_high[pl.ds(image, ROWS), :]
                )
                totals[n % len(totals)][pl.ds(target, ROWS), :] += value
            return carry

        lax.fori_loop(0, (used + UNROLL - 1) // UNROLL, add_group, 0)
        swap = tgt % 2 == 0
        for chip in range(PLANE):
            turned = (chip % NX) * NY + chip // NX
            for core in range(2):
                rows = pl.ds((2 * chip + core) * 16, 16)
                value = totals[0][rows, :]
                for total in totals[1:]:
                    value = value + total[rows, :]
                for total in totals:
                    total[rows, :] = jnp.zeros((16, WIDTH), jnp.float32)
                out[core, position(tgt), jnp.where(swap, turned, chip)] = value
        return carry

    lax.fori_loop(0, NZ, add_list, 0)


def apply(codes, images_low, images_high):
    return pl.pallas_call(
        apply_kernel,
        out_shape=pltpu.VMEM((2, NZ, PLANE, 16, WIDTH), jnp.float32),
        in_specs=[
            pl.BlockSpec(memory_space=pltpu.SMEM),
            pl.BlockSpec(memory_space=pltpu.VMEM),
            pl.BlockSpec(memory_space=pltpu.VMEM),
        ],
        out_specs=pl.BlockSpec(memory_space=pltpu.VMEM),
        scratch_shapes=[pltpu.VMEM((TROWS + 8, WIDTH), jnp.float32)] * 4,
        compiler_params=pltpu.CompilerParams(vmem_limit_bytes=4 * 1024 * 1024),
        name="apply",
    )(codes, images_low, images_high)


def reduce_kernel(
    partial, result, total, partner, wide, narrow, columns,
    local_sem, pair_send, pair_recv, ring_send, ring_recv, tgt_send, tgt_recv,
):
    z, s = lax.axis_index("tgt"), lax.axis_index("src")
    core, chip = lax.rem(s, 2), s // 2
    x, y = lax.rem(chip, NX), chip // NX
    other = s + 1 - 2 * core

    def device(cy, cx):
        return {"src": (lax.rem(cy, NY) * NX + lax.rem(cx, NX)) * 2 + core}

    ahead = (device(y, x + 1), device(y + 1, x))
    behind = (device(y, x + NX - 1), device(y + NY - 1, x))
    across = (device(y, x + 2), device(y + 2, x))
    barrier = pltpu.get_barrier_semaphore()
    peers = [{"src": other}, *ahead, *behind, *across]
    peers += [{"tgt": lax.rem(z + d, NZ)} for d in range(1, NZ)]
    for peer in peers:
        pl.semaphore_signal(barrier, inc=1, device_id=peer, device_id_type=MESH)

    mine = []
    for p in range(PIECES):
        span = pl.ds(p * DEPTH, DEPTH)
        mine.append(pltpu.make_async_copy(
            partial.at[core, span], total.at[span], local_sem.at[p]))
        mine[-1].start()
    pl.semaphore_wait(barrier, len(peers))
    pairs = []
    for p in range(PIECES):
        span = pl.ds(p * DEPTH, DEPTH)
        pairs.append(pltpu.make_async_remote_copy(
            src_ref=partial.at[1 - core, span], dst_ref=partner.at[span],
            send_sem=pair_send.at[p], recv_sem=pair_recv.at[p],
            device_id={"src": other}, device_id_type=MESH,
        ))
        pairs[-1].start()

    here = (x, y)
    pending = []

    def cut(p, level, index, part):
        span = pl.ds(p * DEPTH + part * HALF, HALF)
        return total.at[span, index] if level == 0 else total.at[span, here[p % 2], index]

    def slot(p, level, n):
        return wide.at[p, n] if level == 0 else narrow.at[p, n]

    def send(p, level, n, ref):
        axis = (p + level) % 2
        copy = pltpu.make_async_remote_copy(
            src_ref=ref, dst_ref=slot(p, level, n),
            send_sem=ring_send.at[p, level, n], recv_sem=ring_recv.at[p, level, n],
            device_id=(ahead if n % 2 == 0 else behind)[axis], device_id_type=MESH,
        )
        copy.start()
        pending.append(copy)
        return copy

    rings = {}

    def add(ref, *others):
        value = ref[...]
        for one in others:
            value = value + one[...]
        ref[...] = value

    def first(p, level, near):
        me = here[(p + level) % 2]
        up, far, down = lax.rem(me + 1, 4), lax.rem(me + 2, 4), lax.rem(me + 3, 4)
        ring = rings.setdefault((p, level), {})
        if near:
            ring[2] = send(p, level, 2, cut(p, level, up, 1))
            ring[3] = send(p, level, 3, cut(p, level, down, 0))
        else:
            ring[0] = send(p, level, 0, cut(p, level, far, 0))
            ring[1] = send(p, level, 1, cut(p, level, far, 1))

    def second(p, level):
        me = here[(p + level) % 2]
        up, down = lax.rem(me + 1, 4), lax.rem(me + 3, 4)
        ring = rings[p, level]
        ring[0].wait_recv()
        add(cut(p, level, up, 0), slot(p, level, 0))
        ring[4] = send(p, level, 4, cut(p, level, up, 0))
        ring[1].wait_recv()
        add(cut(p, level, down, 1), slot(p, level, 1))
        ring[5] = send(p, level, 5, cut(p, level, down, 1))

    def third(p, level):
        me = here[(p + level) % 2]
        ring = rings[p, level]
        for n in (2, 3, 4, 5):
            ring[n].wait_recv()
        add(cut(p, level, me, 0), slot(p, level, 3), slot(p, level, 4))
        add(cut(p, level, me, 1), slot(p, level, 2), slot(p, level, 5))

    def begin(p):
        mine[p].wait()
        pairs[p].wait_recv()
        pending.append(pairs[p])

        def one(i, carry):
            total[i] = total[i] + partner[i]
            return carry

        lax.fori_loop(p * DEPTH, (p + 1) * DEPTH, one, 0)
        first(p, 0, False)

    def middle(p):
        third(p, 0)
        axis = (p + 1) % 2
        for n, peer in ((1, ahead), (2, across), (3, behind)):
            copy = pltpu.make_async_remote_copy(
                src_ref=total.at[pl.ds(p * DEPTH, DEPTH), here[p % 2], lax.rem(here[axis] + n, 4)],
                dst_ref=narrow.at[p, n - 1],
                send_sem=ring_send.at[p, 1, n], recv_sem=ring_recv.at[p, 1, n],
                device_id=peer[axis], device_id_type=MESH,
            )
            copy.start()
            pending.append(copy)
            rings[p, 1, n] = copy

    def finish(p):
        for n in (1, 2, 3):
            rings[p, 1, n].wait_recv()
        add(
            total.at[pl.ds(p * DEPTH, DEPTH), here[p % 2], here[(p + 1) % 2]],
            narrow.at[p, 0], narrow.at[p, 1], narrow.at[p, 2],
        )
        for n in range(DEPTH):
            goal = p + n * PIECES

            @pl.when(goal != z)
            def _():
                tgt_copy(goal).start()

    def last(goal):
        swap = goal % 2 == 0
        return total.at[position(goal), jnp.where(swap, x, y), jnp.where(swap, y, x)]

    def tgt_copy(goal):
        shift = lax.rem(goal - z + NZ, NZ) - 1
        return pltpu.make_async_remote_copy(
            src_ref=last(goal), dst_ref=columns.at[z],
            send_sem=tgt_send.at[shift], recv_sem=tgt_recv.at[shift],
            device_id={"tgt": goal}, device_id_type=MESH,
        )

    couples = [(p, p + 1) for p in range(0, PIECES, 2)]
    for n, both in enumerate(couples):
        for p in both:
            begin(p)
        if n > 0:
            for p in couples[n - 1]:
                first(p, 0, True)
    for p in couples[-1]:
        first(p, 0, True)
    for p in range(PIECES):
        second(p, 0)
    for p in range(PIECES):
        middle(p)
    for p in range(PIECES):
        finish(p)
    columns[z] = last(z)[...]
    for copy in pending:
        copy.wait_send()
    for d in range(1, NZ):
        tgt_copy(lax.rem(z + d, NZ)).wait()
    for tgt in range(NZ):
        for n in range(4):
            result[n, pl.ds(tgt * ROWS, ROWS), :] = columns[tgt, pl.ds(n * ROWS, ROWS), :]


def reduce(partial):
    return pl.pallas_call(
        reduce_kernel,
        out_shape=jax.ShapeDtypeStruct((4, NZ * ROWS, WIDTH), jnp.float32),
        in_specs=[pl.BlockSpec(memory_space=pl.ANY)],
        out_specs=pl.BlockSpec(memory_space=pltpu.VMEM),
        scratch_shapes=[
            pltpu.VMEM((NZ, 4, 4, 16, WIDTH), jnp.float32),
            pltpu.VMEM((NZ, 4, 4, 16, WIDTH), jnp.float32),
            pltpu.VMEM((PIECES, 6, HALF, 4, 16, WIDTH), jnp.float32),
            pltpu.VMEM((PIECES, 3, DEPTH, 16, WIDTH), jnp.float32),
            pltpu.VMEM((NZ, 16, WIDTH), jnp.float32),
            pltpu.SemaphoreType.DMA((PIECES,)),
            pltpu.SemaphoreType.DMA((PIECES,)),
            pltpu.SemaphoreType.DMA((PIECES,)),
            pltpu.SemaphoreType.DMA((PIECES, 2, 6)),
            pltpu.SemaphoreType.DMA((PIECES, 2, 6)),
            pltpu.SemaphoreType.DMA((NZ - 1,)),
            pltpu.SemaphoreType.DMA((NZ - 1,)),
        ],
        compiler_params=pltpu.CompilerParams(
            collective_id=1, has_side_effects=True, vmem_limit_bytes=12 * 1024 * 1024
        ),
        name="reduce",
    )(partial)


def on_device(source_coef, couplings, block_list, block_count):
    coef = source_coef.reshape(SOURCES * ROWS, WIDTH)
    codes, low, high = exchange(block_list.reshape(3, 4, 128), block_count, couplings, coef)
    partial = apply(codes.reshape(NZ * 1024), low, high)
    return reduce(partial.reshape(2, NZ, 4, 4, 16, WIDTH))


def solution(mesh):
    in_specs = (
        P("src", "tgt", None),
        P("src", None, None),
        P(None, "tgt", "src", None),
        P("tgt", "src"),
    )
    out_specs = P(("tgt", "src"), None, None)
    return jax.shard_map(
        on_device, mesh=mesh, in_specs=in_specs, out_specs=out_specs, check_vma=False
    )
```

```python
import functools

import jax
import jax.numpy as jnp
from jax import lax
from jax.experimental import pallas as pl
from jax.experimental.pallas import tpu as pltpu
from jax.sharding import PartitionSpec as P

MESH = pl.DeviceIdType.MESH
NX, NY, NZ = 4, 4, 16
PLANE = NX * NY
KINDS, COEF, WIDTH = 64, 64, 128
SOURCES, ROWS = 256, 4
TARGETS, SLOTS = 128, 512
PIECES = 8
DEPTH = NZ // PIECES
HALF = DEPTH // 2
TROWS = TARGETS * ROWS
UNROLL = 32
STRIDE = 528
GROUP = 2
NEAREST = (0, 1, 3, 4, 12, 2, 8, 5, 13, 7, 15, 6, 14, 9, 11, 10)


def position(tgt):
    return (tgt % PIECES) * DEPTH + tgt // PIECES


def exchange_kernel(
    lists_in, count, own, coef_in, codes, images_low, images_high, blocks, packed, spread, inputs,
    lists, coef,
    plane_send, plane_recv, core_send, core_recv, tgt_send, tgt_recv, local_sem,
):
    z, s = lax.axis_index("tgt"), lax.axis_index("src")
    core, chip = lax.rem(s, 2), s // 2
    x, y = lax.rem(chip, NX), chip // NX
    other = s + 1 - 2 * core

    def chip_at(n, sign):
        if isinstance(n, int):
            shift = NEAREST[n]
        else:
            shift = sum(jnp.where(n == m, NEAREST[m], 0) for m in range(1, PLANE))
        dx, dy = sign * (shift % NX), sign * (shift // NX)
        return lax.rem(y + dy + NY, NY) * NX + lax.rem(x + dx + NX, NX)

    load_lists = pltpu.make_async_copy(lists_in, lists, local_sem.at[2])
    load_lists.start()
    keep_blocks = pltpu.make_async_copy(own, blocks.at[pl.ds(2 * s, 2)], local_sem.at[0])
    keep_blocks.start()
    load_coef = pltpu.make_async_copy(coef_in, coef, local_sem.at[3])
    load_coef.start()
    barrier = pltpu.get_barrier_semaphore()
    peers = [{"src": other}]
    peers += [{"src": 2 * chip_at(n, 1) + core} for n in range(1, PLANE)]
    peers += [{"tgt": lax.rem(z + d, NZ)} for d in range(1, NZ)]
    for peer in peers:
        pl.semaphore_signal(barrier, inc=1, device_id=peer, device_id_type=MESH)

    usable = count[0, 0]
    place = (
        lax.broadcasted_iota(jnp.int32, (4, 128), 0) * 128
        + lax.broadcasted_iota(jnp.int32, (4, 128), 1)
    )
    load_lists.wait()
    packed[pl.ds(0, 4), :] = lists[2] * STRIDE + lists[1] * 2
    packed[pl.ds(4, 4), :] = (
        jnp.where(place < usable, lists[0] * ROWS, TROWS)
        + jnp.where(place == 0, usable * 1024, 0)
    )
    keep_codes = pltpu.make_async_copy(packed, codes.at[z], local_sem.at[1])
    keep_codes.start()

    pl.semaphore_wait(barrier, len(peers))

    def plane_copy(n):
        return pltpu.make_async_remote_copy(
            src_ref=own, dst_ref=blocks.at[pl.ds(2 * s, 2)],
            send_sem=plane_send.at[n], recv_sem=plane_recv.at[n],
            device_id={"src": 2 * chip_at(n, 1) + core}, device_id_type=MESH,
        )

    def tgt_copy(d):
        return pltpu.make_async_remote_copy(
            src_ref=packed, dst_ref=codes.at[z],
            send_sem=tgt_send.at[d], recv_sem=tgt_recv.at[d],
            device_id={"tgt": lax.rem(z + d, NZ)}, device_id_type=MESH,
        )

    def core_copy(n):
        owner = pl.ds(4 * chip_at(n, -1) + 2 * core, 2)
        return pltpu.make_async_remote_copy(
            src_ref=blocks.at[owner], dst_ref=blocks.at[owner],
            send_sem=core_send.at[n], recv_sem=core_recv.at[n],
            device_id={"src": other}, device_id_type=MESH,
        )

    for d in range(1, NZ):
        tgt_copy(d).start()
    for n in range(1, PLANE):
        plane_copy(n).start()
    keep_blocks.wait()
    core_copy(0).start()

    load_coef.wait()
    spread[0] = coef[...].astype(jnp.float32)
    spread[1] = jnp.zeros_like(spread[1])
    spread[2] = jnp.zeros_like(spread[2])
    for row in range(ROWS):
        half = row // 2
        spread[1 + half, pl.ds(row, SOURCES, stride=2), :] = spread[
            0, pl.ds(row, SOURCES, stride=ROWS), :
        ]
        if row % 2 == 1:
            inputs[pl.ds(half * STRIDE, STRIDE), :] = (
                spread[1 + half, pl.ds(0, STRIDE), :].astype(jnp.bfloat16))


    sign = jnp.where(
        lax.broadcasted_iota(jnp.int32, (COEF, WIDTH), 1) < COEF, -1.0, 1.0
    ).astype(jnp.float32)

    def square(kind):
        upper = blocks[kind]
        turned = pltpu.roll(upper.astype(jnp.float32), COEF, 1) * sign
        return jnp.concatenate([upper, turned.astype(jnp.bfloat16)], axis=0)

    def build(kinds):
        wide = jnp.concatenate([square(kind) for kind in kinds], axis=1)
        for half, images in enumerate((images_low, images_high)):
            product = jnp.dot(
                inputs[pl.ds(half * STRIDE, STRIDE), :], wide,
                preferred_element_type=jnp.float32,
            )
            for n, kind in enumerate(kinds):
                rows = pl.ds(pl.multiple_of(kind * STRIDE, STRIDE), STRIDE)
                images[rows, :] = product[:, n * WIDTH:(n + 1) * WIDTH]

    def arrive(n):
        if not isinstance(n, int) or n > 0:
            plane_copy(n).wait_recv()
            core_copy(n).start()

    def step(first, own_part, other_part):
        kinds = []
        if own_part:
            for n in range(GROUP):
                arrive(first + n)
                kinds += [4 * chip_at(first + n, -1) + 2 * core + m for m in range(2)]
        if other_part:
            for n in range(GROUP):
                place = first - GROUP + n
                core_copy(place).wait_recv()
                kinds += [4 * chip_at(place, -1) + 2 * (1 - core) + m for m in range(2)]
        build(kinds)

    def both(group, carry):
        step(group * GROUP, True, True)
        return carry

    step(0, True, False)
    lax.fori_loop(1, PLANE // GROUP, both, 0)
    step(PLANE, False, True)
    for d in range(1, NZ):
        tgt_copy(d).wait()
    for n in range(PLANE):
        core_copy(n).wait_send()
    for n in range(1, PLANE):
        plane_copy(n).wait_send()
    keep_codes.wait()


def exchange(lists, count, couplings, coef):
    vmem = pl.BlockSpec(memory_space=pltpu.VMEM)
    hbm = pl.BlockSpec(memory_space=pltpu.HBM)
    lists, couplings, coef = (
        pltpu.with_memory_space_constraint(one, pltpu.HBM) for one in (lists, couplings, coef)
    )
    return pl.pallas_call(
        exchange_kernel,
        out_shape=[
            pltpu.VMEM((NZ, 8, 128), jnp.int32),
            pltpu.VMEM((KINDS * STRIDE, WIDTH), jnp.float32),
            pltpu.VMEM((KINDS * STRIDE, WIDTH), jnp.float32),
        ],
        in_specs=[hbm, pl.BlockSpec(memory_space=pltpu.SMEM), hbm, hbm],
        out_specs=[vmem, vmem, vmem],
        scratch_shapes=[
            pltpu.VMEM((KINDS, COEF, WIDTH), jnp.bfloat16),
            pltpu.VMEM((8, 128), jnp.int32),
            pltpu.VMEM((3, SOURCES * ROWS, WIDTH), jnp.float32),
            pltpu.VMEM((2 * STRIDE, WIDTH), jnp.bfloat16),
            pltpu.VMEM((3, 4, 128), jnp.int32),
            pltpu.VMEM((SOURCES * ROWS, WIDTH), jnp.bfloat16),
            pltpu.SemaphoreType.DMA((PLANE,)),
            pltpu.SemaphoreType.DMA((PLANE,)),
            pltpu.SemaphoreType.DMA((PLANE,)),
            pltpu.SemaphoreType.DMA((PLANE,)),
            pltpu.SemaphoreType.DMA((NZ,)),
            pltpu.SemaphoreType.DMA((NZ,)),
            pltpu.SemaphoreType.DMA((4,)),
        ],
        compiler_params=pltpu.CompilerParams(
            collective_id=0, has_side_effects=True, vmem_limit_bytes=14 * 1024 * 1024
        ),
        name="exchange",
    )(lists, count, couplings, coef)


def apply_kernel(codes_in, images_low, images_high, out, codes, load_sem, *totals):
    def load(tgt):
        words = pl.ds(tgt * 1024, 1024)
        return pltpu.make_async_copy(codes_in.at[words], codes.at[words], load_sem.at[tgt])

    for tgt in range(NZ):
        load(tgt).start()
    low = lax.broadcasted_iota(jnp.int32, (ROWS, WIDTH), 0) < 2

    for total in totals:
        total[...] = jnp.zeros_like(total)

    def add_list(tgt, carry):
        load(tgt).wait()
        base = tgt * 1024
        used = lax.shift_right_logical(codes[base + SLOTS], 10)

        def add_group(group, carry):
            start = base + group * UNROLL
            for n in range(UNROLL):
                image, target = codes[start + n], codes[start + SLOTS + n]
                if n == 0:
                    target = jnp.bitwise_and(target, 1023)
                value = jnp.where(
                    low, images_low[pl.ds(image, ROWS), :], images_high[pl.ds(image, ROWS), :]
                )
                totals[n % len(totals)][pl.ds(target, ROWS), :] += value
            return carry

        lax.fori_loop(0, (used + UNROLL - 1) // UNROLL, add_group, 0)
        swap = tgt % 2 == 0
        for chip in range(PLANE):
            turned = (chip % NX) * NY + chip // NX
            for core in range(2):
                rows = pl.ds((2 * chip + core) * 16, 16)
                value = totals[0][rows, :]
                for total in totals[1:]:
                    value = value + total[rows, :]
                for total in totals:
                    total[rows, :] = jnp.zeros((16, WIDTH), jnp.float32)
                out[core, position(tgt), jnp.where(swap, turned, chip)] = value
        return carry

    lax.fori_loop(0, NZ, add_list, 0)


def apply(codes, images_low, images_high):
    return pl.pallas_call(
        apply_kernel,
        out_shape=pltpu.VMEM((2, NZ, PLANE, 16, WIDTH), jnp.float32),
        in_specs=[
            pl.BlockSpec(memory_space=pl.ANY),
            pl.BlockSpec(memory_space=pltpu.VMEM),
            pl.BlockSpec(memory_space=pltpu.VMEM),
        ],
        out_specs=pl.BlockSpec(memory_space=pltpu.VMEM),
        scratch_shapes=[
            pltpu.SMEM((NZ * 1024,), jnp.int32),
            pltpu.SemaphoreType.DMA((NZ,)),
            *[pltpu.VMEM((TROWS + 8, WIDTH), jnp.float32)] * 4,
        ],
        compiler_params=pltpu.CompilerParams(vmem_limit_bytes=4 * 1024 * 1024),
        name="apply",
    )(codes, images_low, images_high)


def reduce_kernel(
    partial, result, total, partner, wide, narrow, columns,
    local_sem, pair_send, pair_recv, ring_send, ring_recv, tgt_send, tgt_recv,
):
    z, s = lax.axis_index("tgt"), lax.axis_index("src")
    core, chip = lax.rem(s, 2), s // 2
    x, y = lax.rem(chip, NX), chip // NX
    other = s + 1 - 2 * core

    def device(cy, cx):
        return {"src": (lax.rem(cy, NY) * NX + lax.rem(cx, NX)) * 2 + core}

    ahead = (device(y, x + 1), device(y + 1, x))
    behind = (device(y, x + NX - 1), device(y + NY - 1, x))
    across = (device(y, x + 2), device(y + 2, x))
    barrier = pltpu.get_barrier_semaphore()
    peers = [{"src": other}, *ahead, *behind, *across]
    peers += [{"tgt": lax.rem(z + d, NZ)} for d in range(1, NZ)]
    for peer in peers:
        pl.semaphore_signal(barrier, inc=1, device_id=peer, device_id_type=MESH)

    mine = []
    for p in range(PIECES):
        span = pl.ds(p * DEPTH, DEPTH)
        mine.append(pltpu.make_async_copy(
            partial.at[core, span], total.at[span], local_sem.at[p]))
        mine[-1].start()
    pl.semaphore_wait(barrier, len(peers))
    pairs = []
    for p in range(PIECES):
        span = pl.ds(p * DEPTH, DEPTH)
        pairs.append(pltpu.make_async_remote_copy(
            src_ref=partial.at[1 - core, span], dst_ref=partner.at[span],
            send_sem=pair_send.at[p], recv_sem=pair_recv.at[p],
            device_id={"src": other}, device_id_type=MESH,
        ))
        pairs[-1].start()

    here = (x, y)
    pending = []

    def cut(p, level, index, part):
        span = pl.ds(p * DEPTH + part * HALF, HALF)
        return total.at[span, index] if level == 0 else total.at[span, here[p % 2], index]

    def slot(p, level, n):
        return wide.at[p, n] if level == 0 else narrow.at[p, n]

    def send(p, level, n, ref):
        axis = (p + level) % 2
        copy = pltpu.make_async_remote_copy(
            src_ref=ref, dst_ref=slot(p, level, n),
            send_sem=ring_send.at[p, level, n], recv_sem=ring_recv.at[p, level, n],
            device_id=(ahead if n % 2 == 0 else behind)[axis], device_id_type=MESH,
        )
        copy.start()
        pending.append(copy)
        return copy

    rings = {}

    def add(ref, *others):
        value = ref[...]
        for one in others:
            value = value + one[...]
        ref[...] = value

    def first(p, level, near):
        me = here[(p + level) % 2]
        up, far, down = lax.rem(me + 1, 4), lax.rem(me + 2, 4), lax.rem(me + 3, 4)
        ring = rings.setdefault((p, level), {})
        if near:
            ring[2] = send(p, level, 2, cut(p, level, up, 1))
            ring[3] = send(p, level, 3, cut(p, level, down, 0))
        else:
            ring[0] = send(p, level, 0, cut(p, level, far, 0))
            ring[1] = send(p, level, 1, cut(p, level, far, 1))

    def second(p, level):
        me = here[(p + level) % 2]
        up, down = lax.rem(me + 1, 4), lax.rem(me + 3, 4)
        ring = rings[p, level]
        ring[0].wait_recv()
        add(cut(p, level, up, 0), slot(p, level, 0))
        ring[4] = send(p, level, 4, cut(p, level, up, 0))
        ring[1].wait_recv()
        add(cut(p, level, down, 1), slot(p, level, 1))
        ring[5] = send(p, level, 5, cut(p, level, down, 1))

    def third(p, level):
        me = here[(p + level) % 2]
        ring = rings[p, level]
        for n in (2, 3, 4, 5):
            ring[n].wait_recv()
        add(cut(p, level, me, 0), slot(p, level, 3), slot(p, level, 4))
        add(cut(p, level, me, 1), slot(p, level, 2), slot(p, level, 5))

    def begin(p):
        mine[p].wait()
        pairs[p].wait_recv()
        pending.append(pairs[p])

        def one(i, carry):
            total[i] = total[i] + partner[i]
            return carry

        lax.fori_loop(p * DEPTH, (p + 1) * DEPTH, one, 0)
        first(p, 0, False)

    def middle(p):
        third(p, 0)
        axis = (p + 1) % 2
        for n, peer in ((1, ahead), (2, across), (3, behind)):
            copy = pltpu.make_async_remote_copy(
                src_ref=total.at[pl.ds(p * DEPTH, DEPTH), here[p % 2], lax.rem(here[axis] + n, 4)],
                dst_ref=narrow.at[p, n - 1],
                send_sem=ring_send.at[p, 1, n], recv_sem=ring_recv.at[p, 1, n],
                device_id=peer[axis], device_id_type=MESH,
            )
            copy.start()
            pending.append(copy)
            rings[p, 1, n] = copy

    def finish(p):
        for n in (1, 2, 3):
            rings[p, 1, n].wait_recv()
        add(
            total.at[pl.ds(p * DEPTH, DEPTH), here[p % 2], here[(p + 1) % 2]],
            narrow.at[p, 0], narrow.at[p, 1], narrow.at[p, 2],
        )
        for n in range(DEPTH):
            goal = p + n * PIECES

            @pl.when(goal != z)
            def _():
                tgt_copy(goal).start()

    def last(goal):
        swap = goal % 2 == 0
        return total.at[position(goal), jnp.where(swap, x, y), jnp.where(swap, y, x)]

    def tgt_copy(goal):
        shift = lax.rem(goal - z + NZ, NZ) - 1
        return pltpu.make_async_remote_copy(
            src_ref=last(goal), dst_ref=columns.at[z],
            send_sem=tgt_send.at[shift], recv_sem=tgt_recv.at[shift],
            device_id={"tgt": goal}, device_id_type=MESH,
        )

    couples = [(p, p + 1) for p in range(0, PIECES, 2)]
    for n, both in enumerate(couples):
        for p in both:
            begin(p)
        if n > 0:
            for p in couples[n - 1]:
                first(p, 0, True)
    for p in couples[-1]:
        first(p, 0, True)
    for p in range(PIECES):
        second(p, 0)
    for p in range(PIECES):
        middle(p)
    for p in range(PIECES):
        finish(p)
    columns[z] = last(z)[...]
    for d in range(1, NZ):
        tgt_copy(lax.rem(z + d, NZ)).wait_recv()
    for tgt in range(NZ):
        for n in range(4):
            result[n, pl.ds(tgt * ROWS, ROWS), :] = columns[tgt, pl.ds(n * ROWS, ROWS), :]
    for copy in pending:
        copy.wait_send()
    for d in range(1, NZ):
        tgt_copy(lax.rem(z + d, NZ)).wait_send()


def reduce(partial):
    return pl.pallas_call(
        reduce_kernel,
        out_shape=jax.ShapeDtypeStruct((4, NZ * ROWS, WIDTH), jnp.float32),
        in_specs=[pl.BlockSpec(memory_space=pl.ANY)],
        out_specs=pl.BlockSpec(memory_space=pltpu.VMEM),
        scratch_shapes=[
            pltpu.VMEM((NZ, 4, 4, 16, WIDTH), jnp.float32),
            pltpu.VMEM((NZ, 4, 4, 16, WIDTH), jnp.float32),
            pltpu.VMEM((PIECES, 6, HALF, 4, 16, WIDTH), jnp.float32),
            pltpu.VMEM((PIECES, 3, DEPTH, 16, WIDTH), jnp.float32),
            pltpu.VMEM((NZ, 16, WIDTH), jnp.float32),
            pltpu.SemaphoreType.DMA((PIECES,)),
            pltpu.SemaphoreType.DMA((PIECES,)),
            pltpu.SemaphoreType.DMA((PIECES,)),
            pltpu.SemaphoreType.DMA((PIECES, 2, 6)),
            pltpu.SemaphoreType.DMA((PIECES, 2, 6)),
            pltpu.SemaphoreType.DMA((NZ - 1,)),
            pltpu.SemaphoreType.DMA((NZ - 1,)),
        ],
        compiler_params=pltpu.CompilerParams(
            collective_id=1, has_side_effects=True, vmem_limit_bytes=12 * 1024 * 1024
        ),
        name="reduce",
    )(partial)


def on_device(source_coef, couplings, block_list, block_count):
    coef = source_coef.reshape(SOURCES * ROWS, WIDTH)
    codes, low, high = exchange(block_list.reshape(3, 4, 128), block_count, couplings, coef)
    partial = apply(codes.reshape(NZ * 1024), low, high)
    return reduce(partial.reshape(2, NZ, 4, 4, 16, WIDTH))


def solution(mesh):
    in_specs = (
        P("src", "tgt", None),
        P("src", None, None),
        P(None, "tgt", "src", None),
        P("tgt", "src"),
    )
    out_specs = P(("tgt", "src"), None, None)
    return jax.shard_map(
        on_device, mesh=mesh, in_specs=in_specs, out_specs=out_specs, check_vma=False
    )
```

```python
import functools

import jax
import jax.numpy as jnp
from jax import lax
from jax.experimental import pallas as pl
from jax.experimental.pallas import tpu as pltpu
from jax.sharding import PartitionSpec as P

MESH = pl.DeviceIdType.MESH
NX, NY, NZ = 4, 4, 16
PLANE = NX * NY
KINDS, COEF, WIDTH = 64, 64, 128
SOURCES, ROWS = 256, 4
TARGETS, SLOTS = 128, 512
PIECES = 8
DEPTH = NZ // PIECES
HALF = DEPTH // 2
TROWS = TARGETS * ROWS
UNROLL = 32
STRIDE = 528
GROUP = 2
NEAREST = (0, 1, 3, 4, 12, 2, 8, 5, 13, 7, 15, 6, 14, 9, 11, 10)


def position(tgt):
    return (tgt % PIECES) * DEPTH + tgt // PIECES


def exchange_kernel(
    lists_in, count, own, coef_in, codes, images_low, images_high, blocks, packed, spread, inputs,
    lists, coef,
    plane_send, plane_recv, core_send, core_recv, tgt_send, tgt_recv, local_sem,
):
    z, s = lax.axis_index("tgt"), lax.axis_index("src")
    core, chip = lax.rem(s, 2), s // 2
    x, y = lax.rem(chip, NX), chip // NX
    other = s + 1 - 2 * core

    def chip_at(n, sign):
        if isinstance(n, int):
            shift = NEAREST[n]
        else:
            shift = sum(jnp.where(n == m, NEAREST[m], 0) for m in range(1, PLANE))
        dx, dy = sign * (shift % NX), sign * (shift // NX)
        return lax.rem(y + dy + NY, NY) * NX + lax.rem(x + dx + NX, NX)

    load_lists = pltpu.make_async_copy(lists_in, lists, local_sem.at[2])
    load_lists.start()
    keep_blocks = pltpu.make_async_copy(own, blocks.at[pl.ds(2 * s, 2)], local_sem.at[0])
    keep_blocks.start()
    load_coef = pltpu.make_async_copy(coef_in, coef, local_sem.at[3])
    load_coef.start()
    barrier = pltpu.get_barrier_semaphore()
    peers = [{"src": other}]
    peers += [{"src": 2 * chip_at(n, 1) + core} for n in range(1, PLANE)]
    peers += [{"tgt": lax.rem(z + d, NZ)} for d in range(1, NZ)]
    for peer in peers:
        pl.semaphore_signal(barrier, inc=1, device_id=peer, device_id_type=MESH)

    usable = count[0, 0]
    place = (
        lax.broadcasted_iota(jnp.int32, (4, 128), 0) * 128
        + lax.broadcasted_iota(jnp.int32, (4, 128), 1)
    )
    load_lists.wait()
    packed[pl.ds(0, 4), :] = lists[2] * STRIDE + lists[1] * 2
    packed[pl.ds(4, 4), :] = (
        jnp.where(place < usable, lists[0] * ROWS, TROWS)
        + jnp.where(place == 0, usable * 1024, 0)
    )
    keep_codes = pltpu.make_async_copy(packed, codes.at[z], local_sem.at[1])
    keep_codes.start()

    pl.semaphore_wait(barrier, len(peers))

    def plane_copy(n):
        return pltpu.make_async_remote_copy(
            src_ref=own, dst_ref=blocks.at[pl.ds(2 * s, 2)],
            send_sem=plane_send.at[n], recv_sem=plane_recv.at[n],
            device_id={"src": 2 * chip_at(n, 1) + core}, device_id_type=MESH,
        )

    def tgt_copy(d):
        return pltpu.make_async_remote_copy(
            src_ref=packed, dst_ref=codes.at[z],
            send_sem=tgt_send.at[d], recv_sem=tgt_recv.at[d],
            device_id={"tgt": lax.rem(z + d, NZ)}, device_id_type=MESH,
        )

    def core_copy(n):
        owner = pl.ds(4 * chip_at(n, -1) + 2 * core, 2)
        return pltpu.make_async_remote_copy(
            src_ref=blocks.at[owner], dst_ref=blocks.at[owner],
            send_sem=core_send.at[n], recv_sem=core_recv.at[n],
            device_id={"src": other}, device_id_type=MESH,
        )

    for d in range(1, NZ):
        tgt_copy(d).start()
    for n in range(1, PLANE):
        plane_copy(n).start()
    keep_blocks.wait()
    core_copy(0).start()

    load_coef.wait()
    spread[0] = coef[...].astype(jnp.float32)
    spread[1] = jnp.zeros_like(spread[1])
    spread[2] = jnp.zeros_like(spread[2])
    for row in range(ROWS):
        half = row // 2
        spread[1 + half, pl.ds(row, SOURCES, stride=2), :] = spread[
            0, pl.ds(row, SOURCES, stride=ROWS), :
        ]
        if row % 2 == 1:
            inputs[pl.ds(half * STRIDE, STRIDE), :] = (
                spread[1 + half, pl.ds(0, STRIDE), :].astype(jnp.bfloat16))


    sign = jnp.where(
        lax.broadcasted_iota(jnp.int32, (COEF, WIDTH), 1) < COEF, -1.0, 1.0
    ).astype(jnp.float32)

    def square(kind):
        upper = blocks[kind]
        turned = pltpu.roll(upper.astype(jnp.float32), COEF, 1) * sign
        return jnp.concatenate([upper, turned.astype(jnp.bfloat16)], axis=0)

    def build(kinds):
        wide = jnp.concatenate([square(kind) for kind in kinds], axis=1)
        for half, images in enumerate((images_low, images_high)):
            product = jnp.dot(
                inputs[pl.ds(half * STRIDE, STRIDE), :], wide,
                preferred_element_type=jnp.float32,
            )
            for n, kind in enumerate(kinds):
                rows = pl.ds(pl.multiple_of(kind * STRIDE, STRIDE), STRIDE)
                images[rows, :] = product[:, n * WIDTH:(n + 1) * WIDTH]

    def arrive(n):
        if not isinstance(n, int) or n > 0:
            plane_copy(n).wait_recv()
            core_copy(n).start()

    def step(first, own_part, other_part):
        kinds = []
        if own_part:
            for n in range(GROUP):
                arrive(first + n)
                kinds += [4 * chip_at(first + n, -1) + 2 * core + m for m in range(2)]
        if other_part:
            for n in range(GROUP):
                place = first - GROUP + n
                core_copy(place).wait_recv()
                kinds += [4 * chip_at(place, -1) + 2 * (1 - core) + m for m in range(2)]
        build(kinds)

    def both(group, carry):
        step(group * GROUP, True, True)
        return carry

    step(0, True, False)
    lax.fori_loop(1, PLANE // GROUP, both, 0)
    step(PLANE, False, True)
    for d in range(1, NZ):
        tgt_copy(d).wait()
    for n in range(PLANE):
        core_copy(n).wait_send()
    for n in range(1, PLANE):
        plane_copy(n).wait_send()
    keep_codes.wait()


def exchange(lists, count, couplings, coef):
    vmem = pl.BlockSpec(memory_space=pltpu.VMEM)
    hbm = pl.BlockSpec(memory_space=pltpu.HBM)
    lists, couplings, coef = (
        pltpu.with_memory_space_constraint(one, pltpu.HBM) for one in (lists, couplings, coef)
    )
    return pl.pallas_call(
        exchange_kernel,
        out_shape=[
            pltpu.VMEM((NZ, 8, 128), jnp.int32),
            pltpu.VMEM((KINDS * STRIDE, WIDTH), jnp.float32),
            pltpu.VMEM((KINDS * STRIDE, WIDTH), jnp.float32),
        ],
        in_specs=[hbm, pl.BlockSpec(memory_space=pltpu.SMEM), hbm, hbm],
        out_specs=[vmem, vmem, vmem],
        scratch_shapes=[
            pltpu.VMEM((KINDS, COEF, WIDTH), jnp.bfloat16),
            pltpu.VMEM((8, 128), jnp.int32),
            pltpu.VMEM((3, SOURCES * ROWS, WIDTH), jnp.float32),
            pltpu.VMEM((2 * STRIDE, WIDTH), jnp.bfloat16),
            pltpu.VMEM((3, 4, 128), jnp.int32),
            pltpu.VMEM((SOURCES * ROWS, WIDTH), jnp.bfloat16),
            pltpu.SemaphoreType.DMA((PLANE,)),
            pltpu.SemaphoreType.DMA((PLANE,)),
            pltpu.SemaphoreType.DMA((PLANE,)),
            pltpu.SemaphoreType.DMA((PLANE,)),
            pltpu.SemaphoreType.DMA((NZ,)),
            pltpu.SemaphoreType.DMA((NZ,)),
            pltpu.SemaphoreType.DMA((4,)),
        ],
        compiler_params=pltpu.CompilerParams(
            collective_id=0, has_side_effects=True, vmem_limit_bytes=14 * 1024 * 1024
        ),
        name="exchange",
    )(lists, count, couplings, coef)


def apply_kernel(codes_in, images_low, images_high, out, codes, load_sem, *totals):
    def load(tgt):
        words = pl.ds(tgt * 1024, 1024)
        return pltpu.make_async_copy(codes_in.at[words], codes.at[words], load_sem.at[tgt])

    for tgt in range(NZ):
        load(tgt).start()
    low = lax.broadcasted_iota(jnp.int32, (ROWS, WIDTH), 0) < 2

    for total in totals:
        total[...] = jnp.zeros_like(total)

    def add_list(tgt, carry):
        load(tgt).wait()
        base = tgt * 1024
        used = lax.shift_right_logical(codes[base + SLOTS], 10)

        def add_group(group, carry):
            start = base + group * UNROLL
            for n in range(UNROLL):
                image, target = codes[start + n], codes[start + SLOTS + n]
                if n == 0:
                    target = jnp.bitwise_and(target, 1023)
                value = jnp.where(
                    low, images_low[pl.ds(image, ROWS), :], images_high[pl.ds(image, ROWS), :]
                )
                totals[n % len(totals)][pl.ds(target, ROWS), :] += value
            return carry

        lax.fori_loop(0, (used + UNROLL - 1) // UNROLL, add_group, 0)
        swap = tgt % 2 == 0
        for chip in range(PLANE):
            turned = (chip % NX) * NY + chip // NX
            for core in range(2):
                rows = pl.ds((2 * chip + core) * 16, 16)
                value = totals[0][rows, :]
                for total in totals[1:]:
                    value = value + total[rows, :]
                for total in totals:
                    total[rows, :] = jnp.zeros((16, WIDTH), jnp.float32)
                out[core, position(tgt), jnp.where(swap, turned, chip)] = value
        return carry

    lax.fori_loop(0, NZ, add_list, 0)


def apply(codes, images_low, images_high):
    return pl.pallas_call(
        apply_kernel,
        out_shape=pltpu.VMEM((2, NZ, PLANE, 16, WIDTH), jnp.float32),
        in_specs=[
            pl.BlockSpec(memory_space=pl.ANY),
            pl.BlockSpec(memory_space=pltpu.VMEM),
            pl.BlockSpec(memory_space=pltpu.VMEM),
        ],
        out_specs=pl.BlockSpec(memory_space=pltpu.VMEM),
        scratch_shapes=[
            pltpu.SMEM((NZ * 1024,), jnp.int32),
            pltpu.SemaphoreType.DMA((NZ,)),
            *[pltpu.VMEM((TROWS + 8, WIDTH), jnp.float32)] * 4,
        ],
        compiler_params=pltpu.CompilerParams(vmem_limit_bytes=4 * 1024 * 1024),
        name="apply",
    )(codes, images_low, images_high)


def reduce_kernel(
    partial, result, total, partner, wide, narrow, columns,
    local_sem, pair_send, pair_recv, ring_send, ring_recv, tgt_send, tgt_recv,
):
    z, s = lax.axis_index("tgt"), lax.axis_index("src")
    core, chip = lax.rem(s, 2), s // 2
    x, y = lax.rem(chip, NX), chip // NX
    other = s + 1 - 2 * core

    def device(cy, cx):
        return {"src": (lax.rem(cy, NY) * NX + lax.rem(cx, NX)) * 2 + core}

    ahead = (device(y, x + 1), device(y + 1, x))
    behind = (device(y, x + NX - 1), device(y + NY - 1, x))
    across = (device(y, x + 2), device(y + 2, x))
    barrier = pltpu.get_barrier_semaphore()
    peers = [{"src": other}, *ahead, *behind, *across]
    peers += [{"tgt": lax.rem(z + d, NZ)} for d in range(1, NZ)]
    for peer in peers:
        pl.semaphore_signal(barrier, inc=1, device_id=peer, device_id_type=MESH)

    mine = []
    for p in range(PIECES):
        span = pl.ds(p * DEPTH, DEPTH)
        mine.append(pltpu.make_async_copy(
            partial.at[core, span], total.at[span], local_sem.at[p]))
        mine[-1].start()
    pl.semaphore_wait(barrier, len(peers))
    pairs = []
    for p in range(PIECES):
        span = pl.ds(p * DEPTH, DEPTH)
        pairs.append(pltpu.make_async_remote_copy(
            src_ref=partial.at[1 - core, span], dst_ref=partner.at[span],
            send_sem=pair_send.at[p], recv_sem=pair_recv.at[p],
            device_id={"src": other}, device_id_type=MESH,
        ))
        pairs[-1].start()

    here = (x, y)
    pending = []

    def cut(p, level, index, part):
        span = pl.ds(p * DEPTH + part * HALF, HALF)
        return total.at[span, index] if level == 0 else total.at[span, here[p % 2], index]

    def slot(p, level, n):
        return wide.at[p, n] if level == 0 else narrow.at[p, n]

    def send(p, level, n, ref):
        axis = (p + level) % 2
        copy = pltpu.make_async_remote_copy(
            src_ref=ref, dst_ref=slot(p, level, n),
            send_sem=ring_send.at[p, level, n], recv_sem=ring_recv.at[p, level, n],
            device_id=(ahead if n % 2 == 0 else behind)[axis], device_id_type=MESH,
        )
        copy.start()
        pending.append(copy)
        return copy

    rings = {}

    def add(ref, *others):
        value = ref[...]
        for one in others:
            value = value + one[...]
        ref[...] = value

    def first(p, level, near):
        me = here[(p + level) % 2]
        up, far, down = lax.rem(me + 1, 4), lax.rem(me + 2, 4), lax.rem(me + 3, 4)
        ring = rings.setdefault((p, level), {})
        if near:
            ring[2] = send(p, level, 2, cut(p, level, up, 1))
            ring[3] = send(p, level, 3, cut(p, level, down, 0))
        else:
            ring[0] = send(p, level, 0, cut(p, level, far, 0))
            ring[1] = send(p, level, 1, cut(p, level, far, 1))

    def second(p, level):
        me = here[(p + level) % 2]
        up, down = lax.rem(me + 1, 4), lax.rem(me + 3, 4)
        ring = rings[p, level]
        ring[0].wait_recv()
        add(cut(p, level, up, 0), slot(p, level, 0))
        ring[4] = send(p, level, 4, cut(p, level, up, 0))
        ring[1].wait_recv()
        add(cut(p, level, down, 1), slot(p, level, 1))
        ring[5] = send(p, level, 5, cut(p, level, down, 1))

    def third(p, level):
        me = here[(p + level) % 2]
        ring = rings[p, level]
        for n in (2, 3, 4, 5):
            ring[n].wait_recv()
        add(cut(p, level, me, 0), slot(p, level, 3), slot(p, level, 4))
        add(cut(p, level, me, 1), slot(p, level, 2), slot(p, level, 5))

    def begin(p):
        mine[p].wait()
        pairs[p].wait_recv()
        pending.append(pairs[p])

        def one(i, carry):
            total[i] = total[i] + partner[i]
            return carry

        lax.fori_loop(p * DEPTH, (p + 1) * DEPTH, one, 0)
        first(p, 0, False)

    def middle(p):
        third(p, 0)
        axis = (p + 1) % 2
        for n, peer in ((1, ahead), (2, across), (3, behind)):
            copy = pltpu.make_async_remote_copy(
                src_ref=total.at[pl.ds(p * DEPTH, DEPTH), here[p % 2], lax.rem(here[axis] + n, 4)],
                dst_ref=narrow.at[p, n - 1],
                send_sem=ring_send.at[p, 1, n], recv_sem=ring_recv.at[p, 1, n],
                device_id=peer[axis], device_id_type=MESH,
            )
            copy.start()
            pending.append(copy)
            rings[p, 1, n] = copy

    def finish(p):
        for n in (1, 2, 3):
            rings[p, 1, n].wait_recv()
        add(
            total.at[pl.ds(p * DEPTH, DEPTH), here[p % 2], here[(p + 1) % 2]],
            narrow.at[p, 0], narrow.at[p, 1], narrow.at[p, 2],
        )
        for n in range(DEPTH):
            goal = p + n * PIECES

            @pl.when(goal != z)
            def _():
                tgt_copy(goal).start()

    def last(goal):
        swap = goal % 2 == 0
        return total.at[position(goal), jnp.where(swap, x, y), jnp.where(swap, y, x)]

    def tgt_copy(goal):
        shift = lax.rem(goal - z + NZ, NZ) - 1
        return pltpu.make_async_remote_copy(
            src_ref=last(goal), dst_ref=columns.at[z],
            send_sem=tgt_send.at[shift], recv_sem=tgt_recv.at[shift],
            device_id={"tgt": goal}, device_id_type=MESH,
        )

    couples = [(p, p + 1) for p in range(0, PIECES, 2)]
    for both in couples:
        for p in both:
            begin(p)
        for p in both:
            first(p, 0, True)
    for p in range(PIECES):
        second(p, 0)
    for p in range(PIECES):
        middle(p)
    for p in range(PIECES):
        finish(p)
    columns[z] = last(z)[...]
    for d in range(1, NZ):
        tgt_copy(lax.rem(z + d, NZ)).wait_recv()
    for tgt in range(NZ):
        for n in range(4):
            result[n, pl.ds(tgt * ROWS, ROWS), :] = columns[tgt, pl.ds(n * ROWS, ROWS), :]
    for copy in pending:
        copy.wait_send()
    for d in range(1, NZ):
        tgt_copy(lax.rem(z + d, NZ)).wait_send()


def reduce(partial):
    return pl.pallas_call(
        reduce_kernel,
        out_shape=jax.ShapeDtypeStruct((4, NZ * ROWS, WIDTH), jnp.float32),
        in_specs=[pl.BlockSpec(memory_space=pl.ANY)],
        out_specs=pl.BlockSpec(memory_space=pltpu.VMEM),
        scratch_shapes=[
            pltpu.VMEM((NZ, 4, 4, 16, WIDTH), jnp.float32),
            pltpu.VMEM((NZ, 4, 4, 16, WIDTH), jnp.float32),
            pltpu.VMEM((PIECES, 6, HALF, 4, 16, WIDTH), jnp.float32),
            pltpu.VMEM((PIECES, 3, DEPTH, 16, WIDTH), jnp.float32),
            pltpu.VMEM((NZ, 16, WIDTH), jnp.float32),
            pltpu.SemaphoreType.DMA((PIECES,)),
            pltpu.SemaphoreType.DMA((PIECES,)),
            pltpu.SemaphoreType.DMA((PIECES,)),
            pltpu.SemaphoreType.DMA((PIECES, 2, 6)),
            pltpu.SemaphoreType.DMA((PIECES, 2, 6)),
            pltpu.SemaphoreType.DMA((NZ - 1,)),
            pltpu.SemaphoreType.DMA((NZ - 1,)),
        ],
        compiler_params=pltpu.CompilerParams(
            collective_id=1, has_side_effects=True, vmem_limit_bytes=12 * 1024 * 1024
        ),
        name="reduce",
    )(partial)


def on_device(source_coef, couplings, block_list, block_count):
    coef = source_coef.reshape(SOURCES * ROWS, WIDTH)
    codes, low, high = exchange(block_list.reshape(3, 4, 128), block_count, couplings, coef)
    partial = apply(codes.reshape(NZ * 1024), low, high)
    return reduce(partial.reshape(2, NZ, 4, 4, 16, WIDTH))


def solution(mesh):
    in_specs = (
        P("src", "tgt", None),
        P("src", None, None),
        P(None, "tgt", "src", None),
        P("tgt", "src"),
    )
    out_specs = P(("tgt", "src"), None, None)
    return jax.shard_map(
        on_device, mesh=mesh, in_specs=in_specs, out_specs=out_specs, check_vma=False
    )
```
